128 devices in a mesh: gx: 16 (over y, x), gy: 8 (over z, core).
Axes of the slice: x: 4, y: 4, z: 4, core: 2. Of those that a mesh axis runs over, the one named last changes fastest.
Arguments:
- tangent: float32 [32, 16, 256, 128], P('gx', 'gy')
- jacobians: float32 [32, 16, 2, 4, 256, 256], P('gx', 'gy')
- partner_codes: int32 [32, 16, 2, 4], P('gx', 'gy'), may hold values from 0 to 9, as said below
- owner_map: int32 [32, 16, 32], replicated, may hold values from 0 to 127, as said below
Outputs:
- q_owned: float32 [16384, 8, 128], P(('gx', 'gy'))
- r_factor: float32 [128, 128], replicated
The draws below stay inside these ranges and needn't reach their ends.
Inputs may be any that keep to these rules, and one draw needn't show every extreme that they name: `partner_codes`: code c names the cell offset by c // 3 - 1 along the first dimension and c % 3 - 1 along the second; 9 marks an empty slot; slot 0 of every list is 4, the cell itself. `owner_map`: owners are numbered gx index times 8 plus gy index. Every owner receives exactly 128 blocks; each tile sends at most 2 blocks to one owner and exactly 2 to some owner; the counts a tile sends to the 128 owners are the same list for every tile up to order, and each owner receives each count of that list from exactly one tile.
All inputs are finite; a program needn't handle non-finite values.
Results may differ from the reference program's by a relative error of at most 0.0001.
Values sent between devices are 32-bit elements; how exact they have to be, the bound alone decides.
A program may use at most 64 MiB of HBM per device.

```python
import jax
import jax.numpy as jnp
from jax import lax

VEC = 128
CPX = 2
CPY = 2
SWEEPS = 2
SLOTS = 4
BR = 8
ROWS_CELL = 256
NCX = 32
NCY = 16
TILES = 128
BPC = 32
BLK_DEV = 128
BLOCKS = 16384
ROWS = 131072


def draw_tangent(key, part):
    keys = jax.random.split(key, 3)
    shape = (NCX, NCY, ROWS_CELL, VEC)
    base = jnp.clip(jax.random.normal(keys[0], shape, jnp.float32), -4.0, 4.0)
    row_scale = jnp.exp(jax.random.uniform(keys[1], (NCX, NCY, ROWS_CELL, 1), jnp.float32, -1.2, 1.2))
    col_scale = jnp.exp(jax.random.uniform(keys[2], (1, 1, 1, VEC), jnp.float32, -1.2, 1.2))
    along_x = 0.6 + 0.8 * jnp.arange(NCX, dtype=jnp.float32)[:, None, None, None] / NCX
    along_y = 0.6 + 0.8 * jnp.arange(NCY, dtype=jnp.float32)[None, :, None, None] / NCY
    return base * row_scale * col_scale * along_x * along_y


def draw_jacobians(key, part):
    shape = (NCX, NCY, SWEEPS, SLOTS, ROWS_CELL, ROWS_CELL)
    spread = 0.4 * ROWS_CELL ** (-0.5)
    noise = jnp.clip(jax.random.normal(key, shape, jnp.float32), -4.0, 4.0)
    diagonal = jnp.arange(ROWS_CELL)[:, None] == jnp.arange(ROWS_CELL)[None, :]
    first_slot = (jnp.arange(SLOTS) == 0)[:, None, None]
    identity = (diagonal[None, :, :] & first_slot).astype(jnp.float32)
    return identity + spread * noise


def draw_partner_codes(key, part):
    raw_codes = jax.random.randint(key, (NCX, NCY, SWEEPS, SLOTS), 0, 10, jnp.int32)
    first_slot = jnp.arange(SLOTS, dtype=jnp.int32) == 0
    return jnp.where(first_slot, 4, raw_codes).astype(jnp.int32)


def shuffle_one(subkey):
    return jax.random.permutation(subkey, BLK_DEV).astype(jnp.int32)


def draw_owner_map(key, part):
    keys = jax.random.split(key, 5)
    mean_load = BLK_DEV // TILES
    swing = jax.random.randint(keys[0], (TILES // 2,), -mean_load, mean_load + 1, jnp.int32)
    swing = swing.at[0].set(mean_load)
    loads = jnp.stack([mean_load + swing, mean_load - swing], axis=1).reshape(TILES)
    loads = loads[jax.random.permutation(keys[1], TILES)]
    ends = jnp.cumsum(loads)
    places = jnp.arange(BLK_DEV, dtype=jnp.int32)
    step_of = jnp.sum((ends[None, :] <= places[:, None]).astype(jnp.int32), axis=1)
    start_of = jax.random.permutation(keys[2], TILES).astype(jnp.int32)
    label_of = jax.random.permutation(keys[3], TILES).astype(jnp.int32)
    sender = jnp.arange(TILES, dtype=jnp.int32)[:, None]
    chosen = label_of[(start_of[sender] + step_of[None, :]) % TILES]
    shuffles = jax.vmap(shuffle_one)(jax.random.split(keys[4], TILES))
    chosen = jnp.take_along_axis(chosen, shuffles, axis=1)
    grid = chosen.reshape(NCX // CPX, NCY // CPY, CPX, CPY, BPC).transpose(0, 2, 1, 3, 4)
    return grid.reshape(NCX, NCY, BPC).astype(jnp.int32)


def setup_inputs(seed: int = 0) -> dict:
    key_of = jax.random.split(jax.random.key(seed), 5)
    return {
        "tangent": draw_tangent(jax.random.fold_in(key_of[4], 71), 0),
        "jacobians": draw_jacobians(jax.random.fold_in(key_of[4], 71), 0),
        "partner_codes": draw_partner_codes(jax.random.fold_in(key_of[4], 71), 0),
        "owner_map": draw_owner_map(jax.random.fold_in(key_of[4], 71), 0),
    }


FULL_PRECISION = lax.Precision.HIGHEST

def sweep_grid(field_now, jacobians_now, codes_now):
    cells_x = field_now.shape[0]
    cells_y = field_now.shape[1]
    live_mask = codes_now != 9
    codes_safe = jnp.where(live_mask, codes_now, 4)
    index_x = (jnp.arange(cells_x, dtype=jnp.int32)[:, None, None] + codes_safe // 3 - 1) % cells_x
    index_y = (jnp.arange(cells_y, dtype=jnp.int32)[None, :, None] + codes_safe % 3 - 1) % cells_y
    flat_index = (index_x * cells_y + index_y).astype(jnp.int32)
    cell_rows = field_now.reshape((cells_x * cells_y,) + field_now.shape[2:])
    picked = cell_rows[flat_index] * live_mask.astype(field_now.dtype)[..., None, None]
    return jnp.einsum('abkij,abkjv->abiv', jacobians_now, picked, precision=FULL_PRECISION)

def reference(tangent, jacobians, partner_codes, owner_map):
    field_now = tangent
    for sweep_no in range(SWEEPS):
        field_now = sweep_grid(field_now, jacobians[:, :, sweep_no], partner_codes[:, :, sweep_no])
    matrix = field_now.reshape(ROWS, VEC)
    gram_sum = jnp.dot(matrix.T, matrix, precision=FULL_PRECISION) / ROWS
    factor = jnp.linalg.cholesky(gram_sum).T
    q_rows = jax.scipy.linalg.solve_triangular(factor, matrix.T, trans=1, lower=False).T
    blocks = q_rows.reshape(BLOCKS, BR, VEC)
    cell_x = jnp.arange(NCX, dtype=jnp.int32)[:, None, None]
    cell_y = jnp.arange(NCY, dtype=jnp.int32)[None, :, None]
    block_in = jnp.arange(BPC, dtype=jnp.int32)[None, None, :]
    tile_index = cell_x // CPX * (NCY // CPY) + cell_y // CPY
    local_index = (cell_x % CPX * CPY + cell_y % CPY) * BPC + block_in
    sort_key = (owner_map * (TILES * BLK_DEV) + tile_index * BLK_DEV + local_index).astype(jnp.int32)
    arrange = jnp.argsort(sort_key.reshape(-1)).astype(jnp.int32)
    q_owned = blocks[arrange]
    return (q_owned, factor)
```

```python
import jax
import jax.numpy as jnp
from jax import lax
from jax.experimental import pallas as pl
from jax.experimental.pallas import tpu as pltpu
from jax.sharding import PartitionSpec as P

F32 = jnp.float32
BF16 = jnp.bfloat16
I32 = jnp.int32
FULL = lax.Precision.HIGHEST
MESH = pl.DeviceIdType.MESH

GX, GY = 16, 8
TILES = GX * GY
ROWS = 131072
VEC = 128
CELL = 256
SWEEPS = 2
SLOTS = 4
BR = 8
BLK = 128


def dot(a, b, dims=((1,), (0,)), precision=None):
    return lax.dot_general(a, b, (dims, ((), ())), precision=precision, preferred_element_type=F32)


def split(x):
    high = x.astype(BF16)
    low = (x - high.astype(F32)).astype(BF16)
    return high, low


def iota(shape, dim):
    return lax.broadcasted_iota(I32, shape, dim)


def factor(work, r_out, inv_out):
    sub = iota((BR, VEC), 0)
    for blk in range(VEC // BR):
        lo = BR * blk
        left = work[lo : lo + BR, :VEC]
        right = work[lo : lo + BR, VEC:]
        for j in range(BR):
            k = lo + j
            col = jnp.broadcast_to(left[:, k : k + 1], (BR, VEC))
            pivot = jnp.broadcast_to(col[j : j + 1, :], (BR, VEC))
            inv = lax.rsqrt(pivot)
            inv = inv * (1.5 - 0.5 * (pivot * inv) * inv)
            coef = col * inv
            row_l = jnp.broadcast_to(left[j : j + 1, :], (BR, VEC)) * inv
            row_r = jnp.broadcast_to(right[j : j + 1, :], (BR, VEC)) * inv
            left = jnp.where(sub > j, left - coef * row_l, jnp.where(sub == j, row_l, left))
            right = jnp.where(sub > j, right - coef * row_r, jnp.where(sub == j, row_r, right))
        lane = iota((BR, VEC), 1)
        r_out[lo : lo + BR, :] = jnp.where(lane >= sub + lo, left, 0.0)
        inv_out[lo : lo + BR, :] = right
        if lo + BR < VEC:
            both = jnp.concatenate([left, right], axis=1)
            update = dot(left, both, ((0,), (0,)), FULL)
            work[lo + BR :, :] = work[lo + BR :, :] - update[lo + BR :, :]


def kernel(
    tan, jac, codes, owners, q_out, r_out,
    jv, jhi, jlo, ext0, ext1, acc, amat, omv, idxv, idxs,
    gram, rsb, part, gxb, tot, gfull, work, linv, pk, arr,
    loc_sem, jac_sem, hsend, hrecv, ar_send, ar_recv, a2a_send, a2a_recv, idx_sem,
):
    gx = lax.axis_index("gx")
    gy = lax.axis_index("gy")
    me = gx * GY + gy
    core = lax.rem(gy, 2)
    off, on = core, 1 - core
    gx_hi, gx_lo = lax.rem(gx + 1, GX), lax.rem(gx + GX - 1, GX)
    gy_off = lax.rem(gy + 2 * core - 1 + GY, GY)
    gy_on = lax.rem(gy + 1 - 2 * core + GY, GY)

    def halo(s, src, dst, who, role):
        return pltpu.make_async_remote_copy(
            src_ref=src, dst_ref=dst, send_sem=hsend.at[s, role], recv_sem=hrecv.at[s, role],
            device_id=who, device_id_type=MESH,
        )

    def own(s, ext, a, b):
        return tan.at[a * 2 + b] if s == 0 else ext.at[(1 + a) * 4 + 1 + b]

    def own_copies(s, ext):
        cols = (off, on)
        x_copies = [
            (
                halo(s, own(s, ext, 1, cols[k]), ext.at[1 + cols[k]], (gx_hi, gy), k),
                halo(s, own(s, ext, 0, cols[k]), ext.at[12 + 1 + cols[k]], (gx_lo, gy), 2 + k),
            )
            for k in range(2)
        ]
        y_off = [
            halo(s, own(s, ext, a, off), ext.at[(1 + a) * 4 + 3 * on], (gx, gy_off), 4 + a)
            for a in range(2)
        ]
        y_on = [
            halo(s, own(s, ext, a, on), ext.at[(1 + a) * 4 + 3 * off], (gx, gy_on), 6 + a)
            for a in range(2)
        ]
        return x_copies, y_off, y_on

    def corner_copies(s, ext):
        c_off = [
            halo(s, ext.at[12 * side + 1 + off], ext.at[12 * side + 3 * on], (gx, gy_off), 8 + side)
            for side in range(2)
        ]
        c_on = [
            halo(s, ext.at[12 * side + 1 + on], ext.at[12 * side + 3 * off], (gx, gy_on), 10 + side)
            for side in range(2)
        ]
        return c_off, c_on

    exts = (ext0, ext1)
    sent = []

    x_c, y_off, y_on = own_copies(0, ext0)
    for copy in (*x_c[0], *y_off, *x_c[1], *y_on):
        copy.start()
    locals_ = [
        pltpu.make_async_copy(tan.at[c], ext0.at[(1 + c // 2) * 4 + 1 + c % 2], loc_sem.at[c])
        for c in range(4)
    ]
    for copy in locals_:
        copy.start()
    own_copy = pltpu.make_async_copy(owners, omv, loc_sem.at[4])
    own_copy.start()
    jac_copies = [
        pltpu.make_async_copy(jac.at[:, s], jv.at[s], jac_sem.at[s]) for s in range(SWEEPS)
    ]
    for copy in jac_copies:
        copy.start()

    def product(s, cell, slot, field):
        high, low = split(field)
        j_high = jhi[s, cell, slot]
        j_low = jlo[s, cell, slot]
        wide = dot(j_high, jnp.concatenate([high, low], axis=1))
        return wide[:, :VEC] + (wide[:, VEC:] + dot(j_low, high))

    def split_jacobians(s):
        def body(n, carry):
            cell, slot = lax.div(n, SLOTS), lax.rem(n, SLOTS)
            high, low = split(jv[s, cell, slot])
            jhi[s, cell, slot] = high
            jlo[s, cell, slot] = low
            return carry

        lax.fori_loop(0, 4 * SLOTS, body, 0)

    def own_terms(s, ext):
        def body(cell, carry):
            at = (1 + lax.div(cell, 2)) * 4 + 1 + lax.rem(cell, 2)
            acc[cell] = product(s, cell, 0, ext[at])
            return carry

        lax.fori_loop(0, 4, body, 0)

    def routing():
        ones = jnp.ones((32, VEC), BF16)
        mine = (omv[...] == me).astype(F32).astype(BF16)
        per_cell = dot(mine, ones).astype(BF16)
        cell = iota((TILES, 512), 1)
        tile_of = lax.shift_right_logical(cell, 5) * 8 + lax.shift_right_logical(cell & 15, 1)
        pick = (tile_of == iota((TILES, 512), 0)).astype(F32).astype(BF16)
        count = dot(pick, per_cell)
        rows, lanes = iota((TILES, TILES), 0), iota((TILES, TILES), 1)
        tri = (lanes <= rows).astype(F32).astype(BF16)
        ends = dot(tri, count.astype(BF16))
        places = lanes.astype(F32)
        before = (ends <= places).astype(F32)
        tile_at = jnp.sum(before, axis=0, keepdims=True)
        passed = jnp.sum(before * count, axis=0, keepdims=True)
        slot_at = jnp.clip(2.0 * tile_at + places[:1] - passed, 0.0, 2.0 * TILES - 1.0)
        diag = iota((32, 32), 0) == iota((32, 32), 1)
        stack = []
        for c in range(4):
            row = omv[pl.ds((2 * gx + c // 2) * 16 + 2 * gy + c % 2, 1), :].astype(F32)
            stack.append(jnp.where(diag, jnp.broadcast_to(row, (32, 32)), 0.0))
        owner_of = dot(jnp.concatenate(stack, axis=0).astype(BF16), ones)
        hit = owner_of == places
        order = rows.astype(F32)
        first = jnp.min(jnp.where(hit, order, float(BLK - 1)), axis=0, keepdims=True)
        last = jnp.max(jnp.where(hit, order, 0.0), axis=0, keepdims=True)
        table = jnp.concatenate([first, last, slot_at, jnp.zeros((5, VEC), F32)], axis=0)
        idxv[...] = table.astype(I32)
        copy = pltpu.make_async_copy(idxv, idxs, idx_sem)
        copy.start()
        return copy

    idx_copy = None
    for s in range(SWEEPS):
        ext = exts[s]
        sent += [*x_c[0], *x_c[1], *y_off, *y_on]
        if s == 0:
            jac_copies[0].wait()
            split_jacobians(0)
            for copy in locals_:
                copy.wait()
        own_terms(s, ext)
        c_off, c_on = corner_copies(s, ext)
        for copy in x_c[0]:
            copy.wait_recv()
        for copy in c_off:
            copy.start()
        for copy in x_c[1]:
            copy.wait_recv()
        for copy in c_on:
            copy.start()
        sent += [*c_off, *c_on]
        if s == 0:
            jac_copies[1].wait()
            split_jacobians(1)
            own_copy.wait()
            idx_copy = routing()
        for copy in (*y_on, *y_off, *c_on, *c_off):
            copy.wait_recv()

        if s == 0:
            x_c, y_off, y_on = own_copies(1, ext1)
        for n in range(4):
            a, b = n % 2, (off if n < 2 else on)
            cell = a * 2 + b
            total = acc[cell]
            for slot in range(1, SLOTS):
                code = codes[(cell * SWEEPS + s) * SLOTS + slot]
                live = jnp.where(code != 9, 1.0, 0.0).astype(F32)
                safe = jnp.where(code != 9, code, 4)
                step_x = lax.shift_right_logical(safe * 11, 5)
                step_y = safe - 3 * step_x
                field = ext[(a + step_x) * 4 + b + step_y] * live
                total = total + product(s, cell, slot, field)
            if s == 0:
                ext1[(1 + a) * 4 + 1 + b] = total
                if n == 1:
                    for copy in (*x_c[0], *y_off):
                        copy.start()
                if n == 3:
                    for copy in (*x_c[1], *y_on):
                        copy.start()
            else:
                amat[pl.ds(cell * 32, 32)] = total.reshape(32, BR, VEC)

    rows_all = amat[...].reshape(4 * CELL, VEC)
    gram[...] = dot(rows_all, rows_all, ((0,), (0,)), FULL)
    share = VEC // GY

    def to_gy(step, src, dst, phase):
        k = lax.rem(gy + step, GY)
        return pltpu.make_async_remote_copy(
            src_ref=src(k), dst_ref=dst, send_sem=ar_send.at[phase], recv_sem=ar_recv.at[phase],
            device_id=(gx, k), device_id_type=MESH,
        )

    def wait_bytes(ref, sem):
        pltpu.make_async_copy(ref, ref, sem).wait()

    for step in range(1, GY):
        to_gy(step, lambda k: gram.at[pl.ds(k * share, share)], rsb.at[gy], 0).start()
    rsb[gy] = gram[pl.ds(gy * share, share), :]

    idx_copy.wait()

    def pack(o, carry):
        pk[o, 0] = amat[idxs[0, o] & (BLK - 1)]
        pk[o, 1] = amat[idxs[1, o] & (BLK - 1)]
        return carry

    lax.fori_loop(0, TILES // 2, pack, 0, unroll=8)
    wait_bytes(rsb.at[pl.ds(0, GY - 1)], ar_recv.at[0])
    mine = jnp.sum(rsb[...], axis=0)
    part[...] = mine
    for step in range(1, GX):
        pltpu.make_async_remote_copy(
            src_ref=part, dst_ref=gxb.at[gx], send_sem=ar_send.at[1], recv_sem=ar_recv.at[1],
            device_id=(lax.rem(gx + step, GX), gy), device_id_type=MESH,
        ).start()
    gxb[gx] = mine
    lax.fori_loop(TILES // 2, TILES, pack, 0, unroll=8)
    wait_bytes(gxb.at[pl.ds(0, GX - 1)], ar_recv.at[1])
    mine = jnp.sum(gxb[...], axis=0) * (1.0 / ROWS)
    tot[...] = mine
    for step in range(1, GY):
        to_gy(step, lambda k: tot, gfull.at[pl.ds(gy * share, share)], 2).start()
    gfull[pl.ds(gy * share, share), :] = mine
    wait_bytes(gfull.at[pl.ds(0, (GY - 1) * share)], ar_recv.at[2])

    def send(step, carry):
        o = lax.rem(me + step, TILES)
        pltpu.make_async_remote_copy(
            src_ref=pk.at[o], dst_ref=arr.at[me], send_sem=a2a_send, recv_sem=a2a_recv,
            device_id=(lax.div(o, GY), lax.rem(o, GY)), device_id_type=MESH,
        ).start()
        return carry

    lax.fori_loop(1, TILES, send, 0)
    arr[me] = pk[me]

    eye = (iota((VEC, VEC), 0) == iota((VEC, VEC), 1)).astype(F32)
    work[:, :VEC] = gfull[...]
    work[:, VEC:] = eye
    factor(work, r_out, linv)

    wait_bytes(arr.at[pl.ds(0, TILES - 1)], a2a_recv)

    def unpack(p, carry):
        at = idxs[2, p] & (2 * TILES - 1)
        amat[p] = arr[lax.shift_right_logical(at, 1), at & 1]
        return carry

    lax.fori_loop(0, BLK, unpack, 0, unroll=8)
    rows_all = amat[...].reshape(4 * CELL, VEC)
    q_out[...] = dot(rows_all, linv[...], ((1,), (1,)), FULL).reshape(BLK, BR, VEC)

    for copy in sent:
        copy.wait_send()
    wait_bytes(rsb.at[pl.ds(0, GY - 1)], ar_send.at[0])
    wait_bytes(gxb.at[pl.ds(0, GX - 1)], ar_send.at[1])
    wait_bytes(gfull.at[pl.ds(0, (GY - 1) * share)], ar_send.at[2])
    wait_bytes(arr.at[pl.ds(0, TILES - 1)], a2a_send)


def shards(tangent, jacobians, partner_codes, owner_map):
    hbm = pl.BlockSpec(memory_space=pl.ANY)
    vmem = pl.BlockSpec(memory_space=pltpu.VMEM)
    cells = (4, CELL, VEC)
    return pl.pallas_call(
        kernel,
        out_shape=(
            jax.ShapeDtypeStruct((BLK, BR, VEC), F32),
            jax.ShapeDtypeStruct((VEC, VEC), F32),
        ),
        in_specs=[hbm, hbm, pl.BlockSpec(memory_space=pltpu.SMEM), hbm],
        out_specs=(vmem, vmem),
        scratch_shapes=[
            pltpu.VMEM((SWEEPS, 4, SLOTS, CELL, CELL), F32),
            pltpu.VMEM((SWEEPS, 4, SLOTS, CELL, CELL), BF16),
            pltpu.VMEM((SWEEPS, 4, SLOTS, CELL, CELL), BF16),
            pltpu.VMEM((16, CELL, VEC), F32),
            pltpu.VMEM((16, CELL, VEC), F32),
            pltpu.VMEM(cells, F32),
            pltpu.VMEM((BLK, BR, VEC), F32),
            pltpu.VMEM((512, 32), I32),
            pltpu.VMEM((8, VEC), I32),
            pltpu.SMEM((8, VEC), I32),
            pltpu.VMEM((VEC, VEC), F32),
            pltpu.VMEM((GY, VEC // GY, VEC), F32),
            pltpu.VMEM((VEC // GY, VEC), F32),
            pltpu.VMEM((GX, VEC // GY, VEC), F32),
            pltpu.VMEM((VEC // GY, VEC), F32),
            pltpu.VMEM((VEC, VEC), F32),
            pltpu.VMEM((VEC, 2 * VEC), F32),
            pltpu.VMEM((VEC, VEC), F32),
            pltpu.VMEM((TILES, 2, BR, VEC), F32),
            pltpu.VMEM((TILES, 2, BR, VEC), F32),
            pltpu.SemaphoreType.DMA((5,)),
            pltpu.SemaphoreType.DMA((SWEEPS,)),
            pltpu.SemaphoreType.DMA((SWEEPS, 12)),
            pltpu.SemaphoreType.DMA((SWEEPS, 12)),
            pltpu.SemaphoreType.DMA((3,)),
            pltpu.SemaphoreType.DMA((3,)),
            pltpu.SemaphoreType.DMA,
            pltpu.SemaphoreType.DMA,
            pltpu.SemaphoreType.DMA,
        ],
        compiler_params=pltpu.CompilerParams(
            has_side_effects=True, vmem_limit_bytes=52 * 2**20
        ),
    )(
        tangent.reshape(cells),
        jacobians.reshape(4, SWEEPS, SLOTS, CELL, CELL),
        partner_codes.reshape(-1),
        owner_map.reshape(-1, owner_map.shape[2]),
    )


def solution(mesh):
    return jax.shard_map(
        shards,
        mesh=mesh,
        in_specs=(
            P("gx", "gy", None, None),
            P("gx", "gy", None, None, None, None),
            P("gx", "gy", None, None),
            P(),
        ),
        out_specs=(P(("gx", "gy"), None, None), P()),
        check_vma=False,
    )
```

```python
import jax
import jax.numpy as jnp
from jax import lax
from jax.experimental import pallas as pl
from jax.experimental.pallas import tpu as pltpu
from jax.sharding import PartitionSpec as P

F32 = jnp.float32
BF16 = jnp.bfloat16
I32 = jnp.int32
FULL = lax.Precision.HIGHEST
MESH = pl.DeviceIdType.MESH

GX, GY = 16, 8
TILES = GX * GY
ROWS = 131072
VEC = 128
CELL = 256
SWEEPS = 2
SLOTS = 4
BR = 8
BLK = 128


def dot(a, b, dims=((1,), (0,)), precision=None):
    return lax.dot_general(a, b, (dims, ((), ())), precision=precision, preferred_element_type=F32)


def split(x):
    high = x.astype(BF16)
    low = (x - high.astype(F32)).astype(BF16)
    return high, low


def iota(shape, dim):
    return lax.broadcasted_iota(I32, shape, dim)


def spread(x):
    return jnp.broadcast_to(x, (BR, VEC))


def thirds(x):
    high = x.astype(BF16).astype(F32)
    rest = x - high
    mid = rest.astype(BF16).astype(F32)
    low = (rest - mid).astype(BF16).astype(F32)
    return high, mid, low


def outer(left, both):
    h, m, l = thirds(left)
    hh, mm, ll = thirds(both)
    a = jnp.concatenate([h, h, m, h, m, l], axis=0).astype(BF16)
    b = jnp.concatenate([hh, mm, hh, ll, mm, hh], axis=0).astype(BF16)
    return dot(a, b, ((0,), (0,)))


def panel(left, right, lo):
    sub = iota((BR, VEC), 0)
    cols = [spread(left[:, lo + j : lo + j + 1]) for j in range(BR)]
    block = [[spread(cols[j][i : i + 1, :]) for j in range(i + 1)] for i in range(BR)]
    rows_l = [spread(left[i : i + 1, :]) for i in range(BR)]
    rows_r = [spread(right[i : i + 1, :]) for i in range(BR)]
    for j in range(BR):
        pivot = block[j][j]
        inv = lax.rsqrt(pivot)
        inv = inv * (1.5 - 0.5 * (pivot * inv) * inv)
        rows_l[j] = rows_l[j] * inv
        rows_r[j] = rows_r[j] * inv
        below = [block[i][j] * inv if i > j else None for i in range(BR)]
        for i in range(j + 1, BR):
            for k in range(j + 1, i + 1):
                block[i][k] = block[i][k] - below[i] * below[k]
        for i in range(j + 1, BR):
            rows_l[i] = rows_l[i] - below[i] * rows_l[j]
            rows_r[i] = rows_r[i] - below[i] * rows_r[j]
    left, right = rows_l[0], rows_r[0]
    for j in range(1, BR):
        left = jnp.where(sub == j, rows_l[j], left)
        right = jnp.where(sub == j, rows_r[j], right)
    return left, right


def factor(work, r_out, inv_out):
    sub, lane = iota((BR, VEC), 0), iota((BR, VEC), 1)
    for lo in range(0, VEC, BR):
        hi = lo + BR
        left, right = panel(work[lo:hi, :VEC], work[lo:hi, VEC:], lo)
        r_out[lo:hi, :] = jnp.where(lane >= sub + lo, left, 0.0)
        inv_out[lo:hi, :] = right
        if hi < VEC:
            update = outer(left, jnp.concatenate([left, right], axis=1))
            work[hi:, :] = work[hi:, :] - update[hi:, :]


def kernel(
    tan, jac, codes, owners, q_out, r_out,
    jv, jhi, jlo, ext0, ext1, acc, amat, omv, idxv, idxs,
    gram, rsb, part, gxb, tot, gfull, work, linv, pk, arr,
    loc_sem, jac_sem, hsend, hrecv, ar_send, ar_recv, a2a_send, a2a_recv, idx_sem,
    far_x, farther_x, far_y,
):
    gx = lax.axis_index("gx")
    gy = lax.axis_index("gy")
    me = gx * GY + gy
    core = lax.rem(gy, 2)
    off, on = core, 1 - core
    gx_hi, gx_lo = lax.rem(gx + 1, GX), lax.rem(gx + GX - 1, GX)
    gy_off = lax.rem(gy + 2 * core - 1 + GY, GY)
    gy_on = lax.rem(gy + 1 - 2 * core + GY, GY)

    def halo(s, src, dst, who, role):
        return pltpu.make_async_remote_copy(
            src_ref=src, dst_ref=dst, send_sem=hsend.at[s, role], recv_sem=hrecv.at[s, role],
            device_id=who, device_id_type=MESH,
        )

    def own(s, ext, a, b):
        return tan.at[a * 2 + b] if s == 0 else ext.at[(1 + a) * 4 + 1 + b]

    def own_copies(s, ext):
        cols = (off, on)
        x_copies = [
            (
                halo(s, own(s, ext, 1, cols[k]), ext.at[1 + cols[k]], (gx_hi, gy), k),
                halo(s, own(s, ext, 0, cols[k]), ext.at[12 + 1 + cols[k]], (gx_lo, gy), 2 + k),
            )
            for k in range(2)
        ]
        y_off = [
            halo(s, own(s, ext, a, off), ext.at[(1 + a) * 4 + 3 * on], (gx, gy_off), 4 + a)
            for a in range(2)
        ]
        y_on = [
            halo(s, own(s, ext, a, on), ext.at[(1 + a) * 4 + 3 * off], (gx, gy_on), 6 + a)
            for a in range(2)
        ]
        return x_copies, y_off, y_on

    def corner_copies(s, ext):
        c_off = [
            halo(s, ext.at[12 * side + 1 + off], ext.at[12 * side + 3 * on], (gx, gy_off), 8 + side)
            for side in range(2)
        ]
        c_on = [
            halo(s, ext.at[12 * side + 1 + on], ext.at[12 * side + 3 * off], (gx, gy_on), 10 + side)
            for side in range(2)
        ]
        return c_off, c_on

    exts = (ext0, ext1)
    sent = []

    def along_x(step):
        return (lax.rem(gx + step + GX, GX), gy)

    def along_y(step):
        return (gx, lax.rem(gy + step + GY, GY))

    def greet(sem, who):
        for device in who:
            pl.semaphore_signal(sem, inc=1, device_id=device, device_id_type=MESH)

    barrier = pltpu.get_barrier_semaphore()
    greet(barrier, (along_x(1), along_x(-1), along_y(1), along_y(-1)))
    locals_ = [
        pltpu.make_async_copy(tan.at[c], ext0.at[(1 + c // 2) * 4 + 1 + c % 2], loc_sem.at[c])
        for c in range(4)
    ]
    own_copy = pltpu.make_async_copy(owners, omv, loc_sem.at[4])
    jac_copies = [
        pltpu.make_async_copy(jac.at[:, s], jv.at[s], jac_sem.at[s]) for s in range(SWEEPS)
    ]
    for copy in (*locals_, own_copy, *jac_copies):
        copy.start()
    pl.semaphore_wait(barrier, 4)

    x_c, y_off, y_on = own_copies(0, ext0)
    for copy in (*x_c[0], *y_off, *x_c[1], *y_on):
        copy.start()

    def product(s, cell, slot, field):
        high, low = split(field)
        j_high = jhi[s, cell, slot]
        j_low = jlo[s, cell, slot]
        wide = dot(j_high, jnp.concatenate([high, low], axis=1))
        return wide[:, :VEC] + (wide[:, VEC:] + dot(j_low, high))

    def split_jacobians(s):
        def body(n, carry):
            cell, slot = lax.div(n, SLOTS), lax.rem(n, SLOTS)
            high, low = split(jv[s, cell, slot])
            jhi[s, cell, slot] = high
            jlo[s, cell, slot] = low
            return carry

        lax.fori_loop(0, 4 * SLOTS, body, 0)

    def own_terms(s, ext):
        def body(cell, carry):
            at = (1 + lax.div(cell, 2)) * 4 + 1 + lax.rem(cell, 2)
            acc[cell] = product(s, cell, 0, ext[at])
            return carry

        lax.fori_loop(0, 4, body, 0)

    def routing():
        ones = jnp.ones((32, VEC), BF16)
        mine = (omv[...] == me).astype(F32).astype(BF16)
        per_cell = dot(mine, ones).astype(BF16)
        cell = iota((TILES, 512), 1)
        tile_of = lax.shift_right_logical(cell, 5) * 8 + lax.shift_right_logical(cell & 15, 1)
        pick = (tile_of == iota((TILES, 512), 0)).astype(F32).astype(BF16)
        count = dot(pick, per_cell)
        rows, lanes = iota((TILES, TILES), 0), iota((TILES, TILES), 1)
        tri = (lanes <= rows).astype(F32).astype(BF16)
        ends = dot(tri, count.astype(BF16))
        places = lanes.astype(F32)
        before = (ends <= places).astype(F32)
        tile_at = jnp.sum(before, axis=0, keepdims=True)
        passed = jnp.sum(before * count, axis=0, keepdims=True)
        slot_at = jnp.clip(2.0 * tile_at + places[:1] - passed, 0.0, 2.0 * TILES - 1.0)
        diag = iota((32, 32), 0) == iota((32, 32), 1)
        stack = []
        for c in range(4):
            row = omv[pl.ds((2 * gx + c // 2) * 16 + 2 * gy + c % 2, 1), :].astype(F32)
            stack.append(jnp.where(diag, jnp.broadcast_to(row, (32, 32)), 0.0))
        owner_of = dot(jnp.concatenate(stack, axis=0).astype(BF16), ones)
        hit = owner_of == places
        order = rows.astype(F32)
        first = jnp.min(jnp.where(hit, order, float(BLK - 1)), axis=0, keepdims=True)
        last = jnp.max(jnp.where(hit, order, 0.0), axis=0, keepdims=True)
        table = jnp.concatenate([first, last, slot_at, jnp.zeros((5, VEC), F32)], axis=0)
        idxv[...] = table.astype(I32)
        copy = pltpu.make_async_copy(idxv, idxs, idx_sem)
        copy.start()
        return copy

    idx_copy = None
    for s in range(SWEEPS):
        ext = exts[s]
        sent += [*x_c[0], *x_c[1], *y_off, *y_on]
        if s == 0:
            jac_copies[0].wait()
            split_jacobians(0)
            for copy in locals_:
                copy.wait()
        own_terms(s, ext)
        c_off, c_on = corner_copies(s, ext)
        for copy in x_c[0]:
            copy.wait_recv()
        for copy in c_off:
            copy.start()
        for copy in x_c[1]:
            copy.wait_recv()
        for copy in c_on:
            copy.start()
        if s == 0:
            greet(far_x, (along_x(2), along_x(-2)))
        else:
            pl.semaphore_wait(farther_x, 2)
        sent += [*c_off, *c_on]
        if s == 0:
            jac_copies[1].wait()
            split_jacobians(1)
            own_copy.wait()
            idx_copy = routing()
        for copy in (*y_on, *y_off, *c_on, *c_off):
            copy.wait_recv()
        if s == 0:
            pl.semaphore_wait(far_x, 2)
            greet(farther_x, (along_x(4), along_x(-4)))
            greet(far_y, (along_y(2), along_y(-2)))
        else:
            pl.semaphore_wait(far_y, 2)

        if s == 0:
            x_c, y_off, y_on = own_copies(1, ext1)
        for n in range(4):
            a, b = n % 2, (off if n < 2 else on)
            cell = a * 2 + b
            total = acc[cell]
            for slot in range(1, SLOTS):
                code = codes[a, b, s, slot]
                live = jnp.where(code != 9, 1.0, 0.0).astype(F32)
                safe = jnp.where(code != 9, code, 4)
                step_x = lax.shift_right_logical(safe * 11, 5)
                step_y = safe - 3 * step_x
                field = ext[(a + step_x) * 4 + b + step_y] * live
                total = total + product(s, cell, slot, field)
            if s == 0:
                ext1[(1 + a) * 4 + 1 + b] = total
                if n == 1:
                    for copy in (*x_c[0], *y_off):
                        copy.start()
                if n == 3:
                    for copy in (*x_c[1], *y_on):
                        copy.start()
            else:
                amat[pl.ds(cell * 32, 32)] = total.reshape(32, BR, VEC)

    rows_all = amat[...].reshape(4 * CELL, VEC)
    gram[...] = dot(rows_all, rows_all, ((0,), (0,)), FULL)
    share = VEC // GY

    def to_gy(step, src, dst, phase):
        k = lax.rem(gy + step, GY)
        return pltpu.make_async_remote_copy(
            src_ref=src(k), dst_ref=dst, send_sem=ar_send.at[phase], recv_sem=ar_recv.at[phase],
            device_id=(gx, k), device_id_type=MESH,
        )

    def wait_bytes(ref, sem):
        pltpu.make_async_copy(ref, ref, sem).wait()

    for step in range(1, GY):
        to_gy(step, lambda k: gram.at[pl.ds(k * share, share)], rsb.at[gy], 0).start()
    rsb[gy] = gram[pl.ds(gy * share, share), :]

    idx_copy.wait()

    def pack(o, carry):
        pk[o, 0] = amat[idxs[0, o] & (BLK - 1)]
        pk[o, 1] = amat[idxs[1, o] & (BLK - 1)]
        return carry

    def send(step, carry):
        o = lax.rem(me + 37 * step, TILES)
        pltpu.make_async_remote_copy(
            src_ref=pk.at[o], dst_ref=arr.at[me], send_sem=a2a_send, recv_sem=a2a_recv,
            device_id=(lax.div(o, GY), lax.rem(o, GY)), device_id_type=MESH,
        ).start()
        return carry

    lax.fori_loop(0, TILES, pack, 0, unroll=8)
    arr[me] = pk[me]
    wait_bytes(rsb.at[pl.ds(0, GY - 1)], ar_recv.at[0])
    mine = jnp.sum(rsb[...], axis=0)
    part[...] = mine
    for step in range(1, GX):
        pltpu.make_async_remote_copy(
            src_ref=part, dst_ref=gxb.at[gx], send_sem=ar_send.at[1], recv_sem=ar_recv.at[1],
            device_id=(lax.rem(gx + step, GX), gy), device_id_type=MESH,
        ).start()
    gxb[gx] = mine
    lax.fori_loop(1, 49, send, 0)
    wait_bytes(gxb.at[pl.ds(0, GX - 1)], ar_recv.at[1])
    mine = jnp.sum(gxb[...], axis=0) * (1.0 / ROWS)
    tot[...] = mine
    for step in range(1, GY):
        to_gy(step, lambda k: tot, gfull.at[pl.ds(gy * share, share)], 2).start()
    gfull[pl.ds(gy * share, share), :] = mine
    lax.fori_loop(49, 97, send, 0)
    wait_bytes(gfull.at[pl.ds(0, (GY - 1) * share)], ar_recv.at[2])
    lax.fori_loop(97, TILES, send, 0)

    eye = (iota((VEC, VEC), 0) == iota((VEC, VEC), 1)).astype(F32)
    work[:, :VEC] = gfull[...]
    work[:, VEC:] = eye
    factor(work, r_out, linv)

    wait_bytes(arr.at[pl.ds(0, TILES - 1)], a2a_recv)

    def unpack(p, carry):
        at = idxs[2, p] & (2 * TILES - 1)
        amat[p] = arr[lax.shift_right_logical(at, 1), at & 1]
        return carry

    lax.fori_loop(0, BLK, unpack, 0, unroll=8)
    rows_all = amat[...].reshape(4 * CELL, VEC)
    q_out[...] = dot(rows_all, linv[...], ((1,), (1,)), FULL).reshape(BLK, BR, VEC)

    for copy in sent:
        copy.wait_send()
    wait_bytes(rsb.at[pl.ds(0, GY - 1)], ar_send.at[0])
    wait_bytes(gxb.at[pl.ds(0, GX - 1)], ar_send.at[1])
    wait_bytes(gfull.at[pl.ds(0, (GY - 1) * share)], ar_send.at[2])
    wait_bytes(arr.at[pl.ds(0, TILES - 1)], a2a_send)


def shards(tangent, jacobians, partner_codes, owner_map):
    hbm = pl.BlockSpec(memory_space=pltpu.HBM)
    vmem = pl.BlockSpec(memory_space=pltpu.VMEM)
    cells = (4, CELL, VEC)
    return pl.pallas_call(
        kernel,
        out_shape=(
            jax.ShapeDtypeStruct((BLK, BR, VEC), F32),
            jax.ShapeDtypeStruct((VEC, VEC), F32),
        ),
        in_specs=[hbm, hbm, pl.BlockSpec(memory_space=pltpu.SMEM), hbm],
        out_specs=(vmem, vmem),
        scratch_shapes=[
            pltpu.VMEM((SWEEPS, 4, SLOTS, CELL, CELL), F32),
            pltpu.VMEM((SWEEPS, 4, SLOTS, CELL, CELL), BF16),
            pltpu.VMEM((SWEEPS, 4, SLOTS, CELL, CELL), BF16),
            pltpu.VMEM((16, CELL, VEC), F32),
            pltpu.VMEM((16, CELL, VEC), F32),
            pltpu.VMEM(cells, F32),
            pltpu.VMEM((BLK, BR, VEC), F32),
            pltpu.VMEM((512, 32), I32),
            pltpu.VMEM((8, VEC), I32),
            pltpu.SMEM((8, VEC), I32),
            pltpu.VMEM((VEC, VEC), F32),
            pltpu.VMEM((GY, VEC // GY, VEC), F32),
            pltpu.VMEM((VEC // GY, VEC), F32),
            pltpu.VMEM((GX, VEC // GY, VEC), F32),
            pltpu.VMEM((VEC // GY, VEC), F32),
            pltpu.VMEM((VEC, VEC), F32),
            pltpu.VMEM((VEC, 2 * VEC), F32),
            pltpu.VMEM((VEC, VEC), F32),
            pltpu.VMEM((TILES, 2, BR, VEC), F32),
            pltpu.VMEM((TILES, 2, BR, VEC), F32),
            pltpu.SemaphoreType.DMA((5,)),
            pltpu.SemaphoreType.DMA((SWEEPS,)),
            pltpu.SemaphoreType.DMA((SWEEPS, 12)),
            pltpu.SemaphoreType.DMA((SWEEPS, 12)),
            pltpu.SemaphoreType.DMA((3,)),
            pltpu.SemaphoreType.DMA((3,)),
            pltpu.SemaphoreType.DMA,
            pltpu.SemaphoreType.DMA,
            pltpu.SemaphoreType.DMA,
            pltpu.SemaphoreType.REGULAR,
            pltpu.SemaphoreType.REGULAR,
            pltpu.SemaphoreType.REGULAR,
        ],
        compiler_params=pltpu.CompilerParams(
            collective_id=0, has_side_effects=True, vmem_limit_bytes=62 * 2**20
        ),
    )(
        tangent.reshape(cells),
        jacobians.reshape(4, SWEEPS, SLOTS, CELL, CELL),
        partner_codes,
        owner_map.reshape(-1, owner_map.shape[2]),
    )


def solution(mesh):
    return jax.shard_map(
        shards,
        mesh=mesh,
        in_specs=(
            P("gx", "gy", None, None),
            P("gx", "gy", None, None, None, None),
            P("gx", "gy", None, None),
            P(),
        ),
        out_specs=(P(("gx", "gy"), None, None), P()),
        check_vma=False,
    )
```

```python
import jax
import jax.numpy as jnp
from jax import lax
from jax.experimental import pallas as pl
from jax.experimental.pallas import tpu as pltpu
from jax.sharding import PartitionSpec as P

F32 = jnp.float32
BF16 = jnp.bfloat16
I32 = jnp.int32
FULL = lax.Precision.HIGHEST
MESH = pl.DeviceIdType.MESH

GX, GY = 16, 8
TILES = GX * GY
ROWS = 131072
VEC = 128
CELL = 256
SWEEPS = 2
SLOTS = 4
BR = 8
BLK = 128
CUTS = (8, 6, 12)


def dot(a, b, dims=((1,), (0,)), precision=None):
    return lax.dot_general(a, b, (dims, ((), ())), precision=precision, preferred_element_type=F32)


def split(x):
    high = x.astype(BF16)
    low = (x - high.astype(F32)).astype(BF16)
    return high, low


def iota(shape, dim):
    return lax.broadcasted_iota(I32, shape, dim)


def spread(x):
    return jnp.broadcast_to(x, (BR, VEC))


def thirds(x):
    high = x.astype(BF16).astype(F32)
    rest = x - high
    mid = rest.astype(BF16).astype(F32)
    low = (rest - mid).astype(BF16).astype(F32)
    return high, mid, low


def outer(left, both):
    h, m, l = thirds(left)
    hh, mm, ll = thirds(both)
    a = jnp.concatenate([h, h, m, h, m, l], axis=0).astype(BF16)
    b = jnp.concatenate([hh, mm, hh, ll, mm, hh], axis=0).astype(BF16)
    return dot(a, b, ((0,), (0,)))


def panel(left, right, lo):
    sub = iota((BR, VEC), 0)
    cols = [spread(left[:, lo + j : lo + j + 1]) for j in range(BR)]
    block = [[spread(cols[j][i : i + 1, :]) for j in range(i + 1)] for i in range(BR)]
    rows_l = [spread(left[i : i + 1, :]) for i in range(BR)]
    rows_r = [spread(right[i : i + 1, :]) for i in range(BR)]
    for j in range(BR):
        pivot = block[j][j]
        inv = lax.rsqrt(pivot)
        inv = inv * (1.5 - 0.5 * (pivot * inv) * inv)
        rows_l[j] = rows_l[j] * inv
        rows_r[j] = rows_r[j] * inv
        below = [block[i][j] * inv if i > j else None for i in range(BR)]
        for i in range(j + 1, BR):
            for k in range(j + 1, i + 1):
                block[i][k] = block[i][k] - below[i] * below[k]
        for i in range(j + 1, BR):
            rows_l[i] = rows_l[i] - below[i] * rows_l[j]
            rows_r[i] = rows_r[i] - below[i] * rows_r[j]
    left, right = rows_l[0], rows_r[0]
    for j in range(1, BR):
        left = jnp.where(sub == j, rows_l[j], left)
        right = jnp.where(sub == j, rows_r[j], right)
    return left, right


def factor(work, r_out, inv_out):
    sub, lane = iota((BR, VEC), 0), iota((BR, VEC), 1)
    for lo in range(0, VEC, BR):
        hi = lo + BR
        left, right = panel(work[lo:hi, :VEC], work[lo:hi, VEC:], lo)
        r_out[lo:hi, :] = jnp.where(lane >= sub + lo, left, 0.0)
        inv_out[lo:hi, :] = right
        if hi < VEC:
            update = outer(left, jnp.concatenate([left, right], axis=1))
            work[hi:, :] = work[hi:, :] - update[hi:, :]


def kernel(
    tan, jac, codes, owners, q_out, r_out,
    jv, jhi, jlo, ext0, ext1, acc, amat, omv, idxv, idxs,
    gram, rsb, part, gxb, tot, gfull, work, linv, pk, arr,
    loc_sem, jac_sem, hsend, hrecv, ar_send, ar_recv, a2a_send, a2a_recv, idx_sem,
    far_x, farther_x, far_y, near_y,
):
    gx = lax.axis_index("gx")
    gy = lax.axis_index("gy")
    me = gx * GY + gy
    core = lax.rem(gy, 2)
    off, on = core, 1 - core
    gx_hi, gx_lo = lax.rem(gx + 1, GX), lax.rem(gx + GX - 1, GX)
    gy_off = lax.rem(gy + 2 * core - 1 + GY, GY)
    gy_on = lax.rem(gy + 1 - 2 * core + GY, GY)

    def halo(s, src, dst, who, role, half=None):
        if half is not None:
            rows = pl.ds(half * (CELL // 2), CELL // 2)
            src, dst = src.at[rows], dst.at[rows]
        part_no = half or 0
        return pltpu.make_async_remote_copy(
            src_ref=src, dst_ref=dst, send_sem=hsend.at[s, role, part_no],
            recv_sem=hrecv.at[s, role, part_no], device_id=who, device_id_type=MESH,
        )

    def own(s, ext, a, b):
        return tan.at[a * 2 + b] if s == 0 else ext.at[(1 + a) * 4 + 1 + b]

    def own_copies(s, ext):
        x_off, x_on = [
            [
                (
                    halo(s, own(s, ext, 1, col), ext.at[1 + col], (gx_hi, gy), k, half),
                    halo(s, own(s, ext, 0, col), ext.at[12 + 1 + col], (gx_lo, gy), 2 + k, half),
                )
                for half in halves
            ]
            for k, col, halves in ((0, off, (0, 1)), (1, on, (None,)))
        ]
        y_off = [
            halo(s, own(s, ext, a, off), ext.at[(1 + a) * 4 + 3 * on], (gx, gy_off), 4 + a)
            for a in range(2)
        ]
        y_on = [
            halo(s, own(s, ext, a, on), ext.at[(1 + a) * 4 + 3 * off], (gx, gy_on), 6 + a)
            for a in range(2)
        ]
        return x_off, x_on, y_off, y_on

    def corner_copies(s, ext):
        c_off = [
            [
                halo(
                    s, ext.at[12 * side + 1 + off], ext.at[12 * side + 3 * on], (gx, gy_off),
                    8 + side, half,
                )
                for side in range(2)
            ]
            for half in range(2)
        ]
        c_on = [
            halo(s, ext.at[12 * side + 1 + on], ext.at[12 * side + 3 * off], (gx, gy_on), 10 + side)
            for side in range(2)
        ]
        return c_off, c_on

    exts = (ext0, ext1)
    sent = []

    def along_x(step):
        return (lax.rem(gx + step + GX, GX), gy)

    def along_y(step):
        return (gx, lax.rem(gy + step + GY, GY))

    def greet(sem, who):
        for device in who:
            pl.semaphore_signal(sem, inc=1, device_id=device, device_id_type=MESH)

    barrier = pltpu.get_barrier_semaphore()
    greet(barrier, (along_x(1), along_x(-1), along_y(1), along_y(-1)))
    locals_ = [
        pltpu.make_async_copy(tan.at[c], ext0.at[(1 + c // 2) * 4 + 1 + c % 2], loc_sem.at[c])
        for c in range(4)
    ]
    own_copy = pltpu.make_async_copy(owners, omv, loc_sem.at[4])
    jac_copies = [
        pltpu.make_async_copy(jac.at[:, s], jv.at[s], jac_sem.at[s]) for s in range(SWEEPS)
    ]
    for copy in (*locals_, own_copy, *jac_copies):
        copy.start()
    pl.semaphore_wait(barrier, 4)

    x_off, x_on, y_off, y_on = own_copies(0, ext0)
    for copy in (*x_off[0], *x_off[1], *y_off, *x_on[0], *y_on):
        copy.start()

    def product(s, cell, slot, field):
        high, low = split(field)
        j_high = jhi[s, cell, slot]
        j_low = jlo[s, cell, slot]
        wide = dot(j_high, jnp.concatenate([high, low], axis=1))
        return wide[:, :VEC] + (wide[:, VEC:] + dot(j_low, high))

    def split_jacobians(s):
        def body(n, carry):
            cell, slot = lax.div(n, SLOTS), lax.rem(n, SLOTS)
            high, low = split(jv[s, cell, slot])
            jhi[s, cell, slot] = high
            jlo[s, cell, slot] = low
            return carry

        lax.fori_loop(0, 4 * SLOTS, body, 0)

    def own_terms(s, ext):
        def body(cell, carry):
            at = (1 + lax.div(cell, 2)) * 4 + 1 + lax.rem(cell, 2)
            acc[cell] = product(s, cell, 0, ext[at])
            return carry

        lax.fori_loop(0, 4, body, 0)

    def routing():
        ones = jnp.ones((32, VEC), BF16)
        mine = (omv[...] == me).astype(F32).astype(BF16)
        per_cell = dot(mine, ones).astype(BF16)
        cell = iota((TILES, 512), 1)
        tile_of = lax.shift_right_logical(cell, 5) * 8 + lax.shift_right_logical(cell & 15, 1)
        pick = (tile_of == iota((TILES, 512), 0)).astype(F32).astype(BF16)
        count = dot(pick, per_cell)
        rows, lanes = iota((TILES, TILES), 0), iota((TILES, TILES), 1)
        tri = (lanes <= rows).astype(F32).astype(BF16)
        ends = dot(tri, count.astype(BF16))
        places = lanes.astype(F32)
        before = (ends <= places).astype(F32)
        tile_at = jnp.sum(before, axis=0, keepdims=True)
        passed = jnp.sum(before * count, axis=0, keepdims=True)
        slot_at = jnp.clip(2.0 * tile_at + places[:1] - passed, 0.0, 2.0 * TILES - 1.0)
        diag = iota((32, 32), 0) == iota((32, 32), 1)
        stack = []
        for c in range(4):
            row = omv[pl.ds((2 * gx + c // 2) * 16 + 2 * gy + c % 2, 1), :].astype(F32)
            stack.append(jnp.where(diag, jnp.broadcast_to(row, (32, 32)), 0.0))
        owner_of = dot(jnp.concatenate(stack, axis=0).astype(BF16), ones)
        hit = owner_of == places
        order = rows.astype(F32)
        first = jnp.min(jnp.where(hit, order, float(BLK - 1)), axis=0, keepdims=True)
        last = jnp.max(jnp.where(hit, order, 0.0), axis=0, keepdims=True)
        table = jnp.concatenate([first, last, slot_at, jnp.zeros((5, VEC), F32)], axis=0)
        idxv[...] = table.astype(I32)
        copy = pltpu.make_async_copy(idxv, idxs, idx_sem)
        copy.start()
        return copy

    idx_copy = None
    for s in range(SWEEPS):
        ext = exts[s]
        sent += [*x_off[0], *x_off[1], *x_on[0], *y_off, *y_on]
        if s == 0:
            jac_copies[0].wait()
            split_jacobians(0)
            for copy in locals_:
                copy.wait()
        own_terms(s, ext)
        c_off, c_on = corner_copies(s, ext)
        for half in range(2):
            for copy in x_off[half]:
                copy.wait_recv()
            for copy in c_off[half]:
                copy.start()
        for copy in x_on[0]:
            copy.wait_recv()
        for copy in c_on:
            copy.start()
        if s == 0:
            greet(far_x, (along_x(2), along_x(-2)))
        else:
            pl.semaphore_wait(farther_x, 2)
            greet(near_y, (along_y(1), along_y(-1)))
        sent += [*c_off[0], *c_off[1], *c_on]
        if s == 0:
            jac_copies[1].wait()
            split_jacobians(1)
            own_copy.wait()
            idx_copy = routing()
        for copy in (*y_on, *y_off, *c_on, *c_off[0], *c_off[1]):
            copy.wait_recv()
        if s == 0:
            pl.semaphore_wait(far_x, 2)
            greet(farther_x, (along_x(4), along_x(-4)))
            greet(far_y, (along_y(2), along_y(-2)))
        else:
            pl.semaphore_wait(far_y, 2)
            pl.semaphore_wait(near_y, 2)

        if s == 0:
            x_off, x_on, y_off, y_on = own_copies(1, ext1)
        for n in range(4):
            a, b = n % 2, (off if n < 2 else on)
            cell = a * 2 + b
            total = acc[cell]
            for slot in range(1, SLOTS):
                code = codes[a, b, s, slot]
                live = jnp.where(code != 9, 1.0, 0.0).astype(F32)
                safe = jnp.where(code != 9, code, 4)
                step_x = lax.shift_right_logical(safe * 11, 5)
                step_y = safe - 3 * step_x
                field = ext[(a + step_x) * 4 + b + step_y] * live
                total = total + product(s, cell, slot, field)
            if s == 0:
                ext1[(1 + a) * 4 + 1 + b] = total
                if n == 1:
                    for copy in (*x_off[0], *x_off[1], *y_off):
                        copy.start()
                if n == 3:
                    for copy in (*x_on[0], *y_on):
                        copy.start()
            else:
                amat[pl.ds(cell * 32, 32)] = total.reshape(32, BR, VEC)

    rows_all = amat[...].reshape(4 * CELL, VEC)
    gram[...] = dot(rows_all, rows_all, ((0,), (0,)), FULL)
    share = VEC // GY

    def to_gy(step, src, dst, phase):
        k = lax.rem(gy + step, GY)
        return pltpu.make_async_remote_copy(
            src_ref=src(k), dst_ref=dst, send_sem=ar_send.at[phase], recv_sem=ar_recv.at[phase],
            device_id=(gx, k), device_id_type=MESH,
        )

    def wait_bytes(ref, sem):
        pltpu.make_async_copy(ref, ref, sem).wait()

    for step in range(1, GY):
        to_gy(step, lambda k: gram.at[pl.ds(k * share, share)], rsb.at[gy], 0).start()
    rsb[gy] = gram[pl.ds(gy * share, share), :]

    idx_copy.wait()

    def pack(o, carry):
        pk[o, 0] = amat[idxs[0, o] & (BLK - 1)]
        pk[o, 1] = amat[idxs[1, o] & (BLK - 1)]
        return carry

    near, away = (0, 1, GY - 1), tuple(range(2, GY - 1))

    def send(places):
        def body(turn, carry):
            to_x = (gx + 7 * turn) & (GX - 1)
            for step in places:
                to_y = (gy + step) & (GY - 1)
                pltpu.make_async_remote_copy(
                    src_ref=pk.at[to_x * GY + to_y], dst_ref=arr.at[me],
                    send_sem=a2a_send, recv_sem=a2a_recv,
                    device_id=(to_x, to_y), device_id_type=MESH,
                ).start()
            return carry

        return body

    lax.fori_loop(0, TILES, pack, 0, unroll=8)
    arr[me] = pk[me]
    send(near[1:])(0, 0)
    lax.fori_loop(1, CUTS[0], send(near), 0)
    wait_bytes(rsb.at[pl.ds(0, GY - 1)], ar_recv.at[0])
    mine = jnp.sum(rsb[...], axis=0)
    part[...] = mine
    for step in range(1, GX):
        pltpu.make_async_remote_copy(
            src_ref=part, dst_ref=gxb.at[gx], send_sem=ar_send.at[1], recv_sem=ar_recv.at[1],
            device_id=(lax.rem(gx + step, GX), gy), device_id_type=MESH,
        ).start()
    gxb[gx] = mine
    lax.fori_loop(CUTS[0], GX, send(near), 0)
    lax.fori_loop(0, CUTS[1], send(away), 0)
    wait_bytes(gxb.at[pl.ds(0, GX - 1)], ar_recv.at[1])
    mine = jnp.sum(gxb[...], axis=0) * (1.0 / ROWS)
    tot[...] = mine
    for step in range(1, GY):
        to_gy(step, lambda k: tot, gfull.at[pl.ds(gy * share, share)], 2).start()
    gfull[pl.ds(gy * share, share), :] = mine
    lax.fori_loop(CUTS[1], CUTS[2], send(away), 0)
    wait_bytes(gfull.at[pl.ds(0, (GY - 1) * share)], ar_recv.at[2])
    lax.fori_loop(CUTS[2], GX, send(away), 0)

    eye = (iota((VEC, VEC), 0) == iota((VEC, VEC), 1)).astype(F32)
    work[:, :VEC] = gfull[...]
    work[:, VEC:] = eye
    factor(work, r_out, linv)

    wait_bytes(arr.at[pl.ds(0, TILES - 1)], a2a_recv)

    def unpack(p, carry):
        at = idxs[2, p] & (2 * TILES - 1)
        amat[p] = arr[lax.shift_right_logical(at, 1), at & 1]
        return carry

    lax.fori_loop(0, BLK, unpack, 0, unroll=8)
    rows_all = amat[...].reshape(4 * CELL, VEC)
    q_out[...] = dot(rows_all, linv[...], ((1,), (1,)), FULL).reshape(BLK, BR, VEC)

    for copy in sent:
        copy.wait_send()
    wait_bytes(rsb.at[pl.ds(0, GY - 1)], ar_send.at[0])
    wait_bytes(gxb.at[pl.ds(0, GX - 1)], ar_send.at[1])
    wait_bytes(gfull.at[pl.ds(0, (GY - 1) * share)], ar_send.at[2])
    wait_bytes(arr.at[pl.ds(0, TILES - 1)], a2a_send)


def shards(tangent, jacobians, partner_codes, owner_map):
    hbm = pl.BlockSpec(memory_space=pltpu.HBM)
    vmem = pl.BlockSpec(memory_space=pltpu.VMEM)
    cells = (4, CELL, VEC)
    return pl.pallas_call(
        kernel,
        out_shape=(
            jax.ShapeDtypeStruct((BLK, BR, VEC), F32),
            jax.ShapeDtypeStruct((VEC, VEC), F32),
        ),
        in_specs=[hbm, hbm, pl.BlockSpec(memory_space=pltpu.SMEM), hbm],
        out_specs=(vmem, vmem),
        scratch_shapes=[
            pltpu.VMEM((SWEEPS, 4, SLOTS, CELL, CELL), F32),
            pltpu.VMEM((SWEEPS, 4, SLOTS, CELL, CELL), BF16),
            pltpu.VMEM((SWEEPS, 4, SLOTS, CELL, CELL), BF16),
            pltpu.VMEM((16, CELL, VEC), F32),
            pltpu.VMEM((16, CELL, VEC), F32),
            pltpu.VMEM(cells, F32),
            pltpu.VMEM((BLK, BR, VEC), F32),
            pltpu.VMEM((512, 32), I32),
            pltpu.VMEM((8, VEC), I32),
            pltpu.SMEM((8, VEC), I32),
            pltpu.VMEM((VEC, VEC), F32),
            pltpu.VMEM((GY, VEC // GY, VEC), F32),
            pltpu.VMEM((VEC // GY, VEC), F32),
            pltpu.VMEM((GX, VEC // GY, VEC), F32),
            pltpu.VMEM((VEC // GY, VEC), F32),
            pltpu.VMEM((VEC, VEC), F32),
            pltpu.VMEM((VEC, 2 * VEC), F32),
            pltpu.VMEM((VEC, VEC), F32),
            pltpu.VMEM((TILES, 2, BR, VEC), F32),
            pltpu.VMEM((TILES, 2, BR, VEC), F32),
            pltpu.SemaphoreType.DMA((5,)),
            pltpu.SemaphoreType.DMA((SWEEPS,)),
            pltpu.SemaphoreType.DMA((SWEEPS, 12, 2)),
            pltpu.SemaphoreType.DMA((SWEEPS, 12, 2)),
            pltpu.SemaphoreType.DMA((3,)),
            pltpu.SemaphoreType.DMA((3,)),
            pltpu.SemaphoreType.DMA,
            pltpu.SemaphoreType.DMA,
            pltpu.SemaphoreType.DMA,
            pltpu.SemaphoreType.REGULAR,
            pltpu.SemaphoreType.REGULAR,
            pltpu.SemaphoreType.REGULAR,
            pltpu.SemaphoreType.REGULAR,
        ],
        compiler_params=pltpu.CompilerParams(
            collective_id=0, has_side_effects=True, vmem_limit_bytes=62 * 2**20
        ),
    )(
        tangent.reshape(cells),
        jacobians.reshape(4, SWEEPS, SLOTS, CELL, CELL),
        partner_codes,
        owner_map.reshape(-1, owner_map.shape[2]),
    )


def solution(mesh):
    return jax.shard_map(
        shards,
        mesh=mesh,
        in_specs=(
            P("gx", "gy", None, None),
            P("gx", "gy", None, None, None, None),
            P("gx", "gy", None, None),
            P(),
        ),
        out_specs=(P(("gx", "gy"), None, None), P()),
        check_vma=False,
    )
```

```python
import jax
import jax.numpy as jnp
from jax import lax
from jax.experimental import pallas as pl
from jax.experimental.pallas import tpu as pltpu
from jax.sharding import PartitionSpec as P

F32 = jnp.float32
BF16 = jnp.bfloat16
I32 = jnp.int32
FULL = lax.Precision.HIGHEST
MESH = pl.DeviceIdType.MESH

GX, GY = 16, 8
TILES = GX * GY
ROWS = 131072
VEC = 128
CELL = 256
SWEEPS = 2
SLOTS = 4
BR = 8
BLK = 128
CUTS = (12, 5, 12)


def dot(a, b, dims=((1,), (0,)), precision=None):
    return lax.dot_general(a, b, (dims, ((), ())), precision=precision, preferred_element_type=F32)


def split(x):
    high = x.astype(BF16)
    low = (x - high.astype(F32)).astype(BF16)
    return high, low


def iota(shape, dim):
    return lax.broadcasted_iota(I32, shape, dim)


def spread(x):
    return jnp.broadcast_to(x, (BR, VEC))


def thirds(x):
    high = x.astype(BF16).astype(F32)
    rest = x - high
    mid = rest.astype(BF16).astype(F32)
    low = (rest - mid).astype(BF16).astype(F32)
    return high, mid, low


def outer(left, both):
    h, m, l = thirds(left)
    hh, mm, ll = thirds(both)
    a = jnp.concatenate([h, h, m, h, m, l], axis=0).astype(BF16)
    b = jnp.concatenate([hh, mm, hh, ll, mm, hh], axis=0).astype(BF16)
    return dot(a, b, ((0,), (0,)))


def panel(left, right, lo):
    sub = iota((BR, VEC), 0)
    cols = [spread(left[:, lo + j : lo + j + 1]) for j in range(BR)]
    block = [[spread(cols[j][i : i + 1, :]) for j in range(i + 1)] for i in range(BR)]
    rows_l = [spread(left[i : i + 1, :]) for i in range(BR)]
    rows_r = [spread(right[i : i + 1, :]) for i in range(BR)]
    for j in range(BR):
        pivot = block[j][j]
        inv = lax.rsqrt(pivot)
        inv = inv * (1.5 - 0.5 * (pivot * inv) * inv)
        rows_l[j] = rows_l[j] * inv
        rows_r[j] = rows_r[j] * inv
        below = [block[i][j] * inv if i > j else None for i in range(BR)]
        for i in range(j + 1, BR):
            for k in range(j + 1, i + 1):
                block[i][k] = block[i][k] - below[i] * below[k]
        for i in range(j + 1, BR):
            rows_l[i] = rows_l[i] - below[i] * rows_l[j]
            rows_r[i] = rows_r[i] - below[i] * rows_r[j]
    left, right = rows_l[0], rows_r[0]
    for j in range(1, BR):
        left = jnp.where(sub == j, rows_l[j], left)
        right = jnp.where(sub == j, rows_r[j], right)
    return left, right


def factor(work, r_out, inv_out):
    sub, lane = iota((BR, VEC), 0), iota((BR, VEC), 1)
    for lo in range(0, VEC, BR):
        hi = lo + BR
        left, right = panel(work[lo:hi, :VEC], work[lo:hi, VEC:], lo)
        r_out[lo:hi, :] = jnp.where(lane >= sub + lo, left, 0.0)
        inv_out[lo:hi, :] = right
        if hi < VEC:
            update = outer(left, jnp.concatenate([left, right], axis=1))
            work[hi:, :] = work[hi:, :] - update[hi:, :]


def kernel(
    tan, jac, codes, owners, q_out, r_out,
    jv, jhi, jlo, ext0, ext1, acc, amat, omv, idxv, idxs,
    gram, rsb, part, gyb, tot, gfull, work, linv, pk, arr,
    loc_sem, jac_sem, hsend, hrecv, ar_send, ar_recv, a2a_send, a2a_recv, idx_sem,
    far_x, farther_x, far_y, near_y,
):
    gx = lax.axis_index("gx")
    gy = lax.axis_index("gy")
    me = gx * GY + gy
    core = lax.rem(gy, 2)
    off, on = core, 1 - core
    gx_hi, gx_lo = lax.rem(gx + 1, GX), lax.rem(gx + GX - 1, GX)
    gy_off = lax.rem(gy + 2 * core - 1 + GY, GY)
    gy_on = lax.rem(gy + 1 - 2 * core + GY, GY)

    def halo(s, src, dst, who, role, half=None):
        if half is not None:
            rows = pl.ds(half * (CELL // 2), CELL // 2)
            src, dst = src.at[rows], dst.at[rows]
        part_no = half or 0
        return pltpu.make_async_remote_copy(
            src_ref=src, dst_ref=dst, send_sem=hsend.at[s, role, part_no],
            recv_sem=hrecv.at[s, role, part_no], device_id=who, device_id_type=MESH,
        )

    def own(s, ext, a, b):
        return tan.at[a * 2 + b] if s == 0 else ext.at[(1 + a) * 4 + 1 + b]

    def own_copies(s, ext):
        x_off, x_on = [
            [
                (
                    halo(s, own(s, ext, 1, col), ext.at[1 + col], (gx_hi, gy), k, half),
                    halo(s, own(s, ext, 0, col), ext.at[12 + 1 + col], (gx_lo, gy), 2 + k, half),
                )
                for half in halves
            ]
            for k, col, halves in ((0, off, (0, 1)), (1, on, (None,)))
        ]
        y_off = [
            halo(s, own(s, ext, a, off), ext.at[(1 + a) * 4 + 3 * on], (gx, gy_off), 4 + a)
            for a in range(2)
        ]
        y_on = [
            halo(s, own(s, ext, a, on), ext.at[(1 + a) * 4 + 3 * off], (gx, gy_on), 6 + a)
            for a in range(2)
        ]
        return x_off, x_on, y_off, y_on

    def corner_copies(s, ext):
        c_off = [
            [
                halo(
                    s, ext.at[12 * side + 1 + off], ext.at[12 * side + 3 * on], (gx, gy_off),
                    8 + side, half,
                )
                for side in range(2)
            ]
            for half in range(2)
        ]
        c_on = [
            halo(s, ext.at[12 * side + 1 + on], ext.at[12 * side + 3 * off], (gx, gy_on), 10 + side)
            for side in range(2)
        ]
        return c_off, c_on

    exts = (ext0, ext1)
    sent = []

    def along_x(step):
        return (lax.rem(gx + step + GX, GX), gy)

    def along_y(step):
        return (gx, lax.rem(gy + step + GY, GY))

    def greet(sem, who):
        for device in who:
            pl.semaphore_signal(sem, inc=1, device_id=device, device_id_type=MESH)

    barrier = pltpu.get_barrier_semaphore()
    greet(barrier, (along_x(1), along_x(-1), along_y(1), along_y(-1)))
    locals_ = [
        pltpu.make_async_copy(tan.at[c], ext0.at[(1 + c // 2) * 4 + 1 + c % 2], loc_sem.at[c])
        for c in range(4)
    ]
    own_copy = pltpu.make_async_copy(owners, omv, loc_sem.at[4])
    jac_copies = [
        pltpu.make_async_copy(jac.at[:, s], jv.at[s], jac_sem.at[s]) for s in range(SWEEPS)
    ]
    for copy in (*locals_, own_copy, *jac_copies):
        copy.start()
    pl.semaphore_wait(barrier, 4)

    x_off, x_on, y_off, y_on = own_copies(0, ext0)
    for copy in (*x_off[0], *x_off[1], *y_off, *x_on[0], *y_on):
        copy.start()

    def product(s, cell, slot, field):
        high, low = split(field)
        j_high = jhi[s, cell, slot]
        j_low = jlo[s, cell, slot]
        wide = dot(j_high, jnp.concatenate([high, low], axis=1))
        return wide[:, :VEC] + (wide[:, VEC:] + dot(j_low, high))

    def split_jacobians(s):
        def body(n, carry):
            cell, slot = lax.div(n, SLOTS), lax.rem(n, SLOTS)
            high, low = split(jv[s, cell, slot])
            jhi[s, cell, slot] = high
            jlo[s, cell, slot] = low
            return carry

        lax.fori_loop(0, 4 * SLOTS, body, 0)

    def own_terms(s, ext):
        def body(cell, carry):
            at = (1 + lax.div(cell, 2)) * 4 + 1 + lax.rem(cell, 2)
            acc[cell] = product(s, cell, 0, ext[at])
            return carry

        lax.fori_loop(0, 4, body, 0)

    def routing():
        ones = jnp.ones((32, VEC), BF16)
        mine = (omv[...] == me).astype(F32).astype(BF16)
        per_cell = dot(mine, ones).astype(BF16)
        cell = iota((TILES, 512), 1)
        tile_of = lax.shift_right_logical(cell, 5) * 8 + lax.shift_right_logical(cell & 15, 1)
        pick = (tile_of == iota((TILES, 512), 0)).astype(F32).astype(BF16)
        count = dot(pick, per_cell)
        rows, lanes = iota((TILES, TILES), 0), iota((TILES, TILES), 1)
        tri = (lanes <= rows).astype(F32).astype(BF16)
        ends = dot(tri, count.astype(BF16))
        places = lanes.astype(F32)
        before = (ends <= places).astype(F32)
        tile_at = jnp.sum(before, axis=0, keepdims=True)
        passed = jnp.sum(before * count, axis=0, keepdims=True)
        slot_at = jnp.clip(2.0 * tile_at + places[:1] - passed, 0.0, 2.0 * TILES - 1.0)
        diag = iota((32, 32), 0) == iota((32, 32), 1)
        stack = []
        for c in range(4):
            row = omv[pl.ds((2 * gx + c // 2) * 16 + 2 * gy + c % 2, 1), :].astype(F32)
            stack.append(jnp.where(diag, jnp.broadcast_to(row, (32, 32)), 0.0))
        owner_of = dot(jnp.concatenate(stack, axis=0).astype(BF16), ones)
        hit = owner_of == places
        order = rows.astype(F32)
        first = jnp.min(jnp.where(hit, order, float(BLK - 1)), axis=0, keepdims=True)
        last = jnp.max(jnp.where(hit, order, 0.0), axis=0, keepdims=True)
        table = jnp.concatenate([first, last, slot_at, jnp.zeros((5, VEC), F32)], axis=0)
        idxv[...] = table.astype(I32)
        copy = pltpu.make_async_copy(idxv, idxs, idx_sem)
        copy.start()
        return copy

    idx_copy = None
    for s in range(SWEEPS):
        ext = exts[s]
        sent += [*x_off[0], *x_off[1], *x_on[0], *y_off, *y_on]
        if s == 0:
            jac_copies[0].wait()
            split_jacobians(0)
            for copy in locals_:
                copy.wait()
        own_terms(s, ext)
        c_off, c_on = corner_copies(s, ext)
        for half in range(2):
            for copy in x_off[half]:
                copy.wait_recv()
            for copy in c_off[half]:
                copy.start()
        for copy in x_on[0]:
            copy.wait_recv()
        for copy in c_on:
            copy.start()
        if s == 0:
            greet(far_x, (along_x(2), along_x(-2)))
        else:
            pl.semaphore_wait(farther_x, 2)
            greet(near_y, (along_y(1), along_y(-1)))
        sent += [*c_off[0], *c_off[1], *c_on]
        if s == 0:
            jac_copies[1].wait()
            split_jacobians(1)
            own_copy.wait()
            idx_copy = routing()
        for copy in (*y_on, *y_off, *c_on, *c_off[0], *c_off[1]):
            copy.wait_recv()
        if s == 0:
            pl.semaphore_wait(far_x, 2)
            greet(farther_x, (along_x(4), along_x(-4)))
            greet(far_y, (along_y(2), along_y(-2)))
        else:
            pl.semaphore_wait(far_y, 2)
            pl.semaphore_wait(near_y, 2)

        if s == 0:
            x_off, x_on, y_off, y_on = own_copies(1, ext1)
        for n in range(4):
            a, b = n % 2, (off if n < 2 else on)
            cell = a * 2 + b
            total = acc[cell]
            for slot in range(1, SLOTS):
                code = codes[a, b, s, slot]
                live = jnp.where(code != 9, 1.0, 0.0).astype(F32)
                safe = jnp.where(code != 9, code, 4)
                step_x = lax.shift_right_logical(safe * 11, 5)
                step_y = safe - 3 * step_x
                field = ext[(a + step_x) * 4 + b + step_y] * live
                total = total + product(s, cell, slot, field)
            if s == 0:
                ext1[(1 + a) * 4 + 1 + b] = total
                if n == 1:
                    for copy in (*x_off[0], *x_off[1], *y_off):
                        copy.start()
                if n == 3:
                    for copy in (*x_on[0], *y_on):
                        copy.start()
            else:
                amat[pl.ds(cell * 32, 32)] = total.reshape(32, BR, VEC)

    rows_all = amat[...].reshape(4 * CELL, VEC)
    gram[...] = dot(rows_all, rows_all, ((0,), (0,)), FULL)
    share = VEC // GX

    def to_gx(step, src, dst, phase):
        k = lax.rem(gx + step, GX)
        return pltpu.make_async_remote_copy(
            src_ref=src(k), dst_ref=dst, send_sem=ar_send.at[phase], recv_sem=ar_recv.at[phase],
            device_id=(k, gy), device_id_type=MESH,
        )

    def wait_bytes(ref, sem):
        pltpu.make_async_copy(ref, ref, sem).wait()

    for step in range(1, GX):
        to_gx(step, lambda k: gram.at[pl.ds(k * share, share)], rsb.at[gx], 0).start()
    rsb[gx] = gram[pl.ds(gx * share, share), :]

    idx_copy.wait()

    def pack(o, carry):
        pk[o, 0] = amat[idxs[0, o] & (BLK - 1)]
        pk[o, 1] = amat[idxs[1, o] & (BLK - 1)]
        return carry

    near, away = (0, 1, GY - 1), tuple(range(2, GY - 1))

    def send(places):
        def body(turn, carry):
            to_x = (gx + 7 * turn) & (GX - 1)
            for step in places:
                to_y = (gy + step) & (GY - 1)
                pltpu.make_async_remote_copy(
                    src_ref=pk.at[to_x * GY + to_y], dst_ref=arr.at[me],
                    send_sem=a2a_send, recv_sem=a2a_recv,
                    device_id=(to_x, to_y), device_id_type=MESH,
                ).start()
            return carry

        return body

    lax.fori_loop(0, TILES, pack, 0, unroll=8)
    arr[me] = pk[me]
    send(near[1:])(0, 0)
    lax.fori_loop(1, CUTS[0], send(near), 0)
    wait_bytes(rsb.at[pl.ds(0, GX - 1)], ar_recv.at[0])
    mine = jnp.sum(rsb[...], axis=0)
    part[...] = mine
    for step in range(1, GY):
        pltpu.make_async_remote_copy(
            src_ref=part, dst_ref=gyb.at[gy], send_sem=ar_send.at[1], recv_sem=ar_recv.at[1],
            device_id=(gx, lax.rem(gy + step, GY)), device_id_type=MESH,
        ).start()
    gyb[gy] = mine
    lax.fori_loop(CUTS[0], GX, send(near), 0)
    lax.fori_loop(0, CUTS[1], send(away), 0)
    wait_bytes(gyb.at[pl.ds(0, GY - 1)], ar_recv.at[1])
    mine = jnp.sum(gyb[...], axis=0) * (1.0 / ROWS)
    tot[...] = mine
    for step in range(1, GX):
        to_gx(step, lambda k: tot, gfull.at[pl.ds(gx * share, share)], 2).start()
    gfull[pl.ds(gx * share, share), :] = mine
    lax.fori_loop(CUTS[1], CUTS[2], send(away), 0)
    wait_bytes(gfull.at[pl.ds(0, (GX - 1) * share)], ar_recv.at[2])
    lax.fori_loop(CUTS[2], GX, send(away), 0)

    eye = (iota((VEC, VEC), 0) == iota((VEC, VEC), 1)).astype(F32)
    work[:, :VEC] = gfull[...]
    work[:, VEC:] = eye
    factor(work, r_out, linv)

    wait_bytes(arr.at[pl.ds(0, TILES - 1)], a2a_recv)

    def unpack(p, carry):
        at = idxs[2, p] & (2 * TILES - 1)
        amat[p] = arr[lax.shift_right_logical(at, 1), at & 1]
        return carry

    lax.fori_loop(0, BLK, unpack, 0, unroll=8)
    rows_all = amat[...].reshape(4 * CELL, VEC)
    q_out[...] = dot(rows_all, linv[...], ((1,), (1,)), FULL).reshape(BLK, BR, VEC)

    for copy in sent:
        copy.wait_send()
    wait_bytes(rsb.at[pl.ds(0, GX - 1)], ar_send.at[0])
    wait_bytes(gyb.at[pl.ds(0, GY - 1)], ar_send.at[1])
    wait_bytes(gfull.at[pl.ds(0, (GX - 1) * share)], ar_send.at[2])
    wait_bytes(arr.at[pl.ds(0, TILES - 1)], a2a_send)


def shards(tangent, jacobians, partner_codes, owner_map):
    hbm = pl.BlockSpec(memory_space=pltpu.HBM)
    vmem = pl.BlockSpec(memory_space=pltpu.VMEM)
    cells = (4, CELL, VEC)
    return pl.pallas_call(
        kernel,
        out_shape=(
            jax.ShapeDtypeStruct((BLK, BR, VEC), F32),
            jax.ShapeDtypeStruct((VEC, VEC), F32),
        ),
        in_specs=[hbm, hbm, pl.BlockSpec(memory_space=pltpu.SMEM), hbm],
        out_specs=(vmem, vmem),
        scratch_shapes=[
            pltpu.VMEM((SWEEPS, 4, SLOTS, CELL, CELL), F32),
            pltpu.VMEM((SWEEPS, 4, SLOTS, CELL, CELL), BF16),
            pltpu.VMEM((SWEEPS, 4, SLOTS, CELL, CELL), BF16),
            pltpu.VMEM((16, CELL, VEC), F32),
            pltpu.VMEM((16, CELL, VEC), F32),
            pltpu.VMEM(cells, F32),
            pltpu.VMEM((BLK, BR, VEC), F32),
            pltpu.VMEM((512, 32), I32),
            pltpu.VMEM((8, VEC), I32),
            pltpu.SMEM((8, VEC), I32),
            pltpu.VMEM((VEC, VEC), F32),
            pltpu.VMEM((GX, VEC // GX, VEC), F32),
            pltpu.VMEM((VEC // GX, VEC), F32),
            pltpu.VMEM((GY, VEC // GX, VEC), F32),
            pltpu.VMEM((VEC // GX, VEC), F32),
            pltpu.VMEM((VEC, VEC), F32),
            pltpu.VMEM((VEC, 2 * VEC), F32),
            pltpu.VMEM((VEC, VEC), F32),
            pltpu.VMEM((TILES, 2, BR, VEC), F32),
            pltpu.VMEM((TILES, 2, BR, VEC), F32),
            pltpu.SemaphoreType.DMA((5,)),
            pltpu.SemaphoreType.DMA((SWEEPS,)),
            pltpu.SemaphoreType.DMA((SWEEPS, 12, 2)),
            pltpu.SemaphoreType.DMA((SWEEPS, 12, 2)),
            pltpu.SemaphoreType.DMA((3,)),
            pltpu.SemaphoreType.DMA((3,)),
            pltpu.SemaphoreType.DMA,
            pltpu.SemaphoreType.DMA,
            pltpu.SemaphoreType.DMA,
            pltpu.SemaphoreType.REGULAR,
            pltpu.SemaphoreType.REGULAR,
            pltpu.SemaphoreType.REGULAR,
            pltpu.SemaphoreType.REGULAR,
        ],
        compiler_params=pltpu.CompilerParams(
            collective_id=0, has_side_effects=True, vmem_limit_bytes=62 * 2**20
        ),
    )(
        tangent.reshape(cells),
        jacobians.reshape(4, SWEEPS, SLOTS, CELL, CELL),
        partner_codes,
        owner_map.reshape(-1, owner_map.shape[2]),
    )


def solution(mesh):
    return jax.shard_map(
        shards,
        mesh=mesh,
        in_specs=(
            P("gx", "gy", None, None),
            P("gx", "gy", None, None, None, None),
            P("gx", "gy", None, None),
            P(),
        ),
        out_specs=(P(("gx", "gy"), None, None), P()),
        check_vma=False,
    )
```

```python
import jax
import jax.numpy as jnp
from jax import lax
from jax.experimental import pallas as pl
from jax.experimental.pallas import tpu as pltpu
from jax.sharding import PartitionSpec as P

F32 = jnp.float32
BF16 = jnp.bfloat16
I32 = jnp.int32
FULL = lax.Precision.HIGHEST
MESH = pl.DeviceIdType.MESH

GX, GY = 16, 8
TILES = GX * GY
ROWS = 131072
VEC = 128
CELL = 256
SWEEPS = 2
SLOTS = 4
BR = 8
BLK = 128
CUTS = (12, 5, 12)


def dot(a, b, dims=((1,), (0,)), precision=None):
    return lax.dot_general(a, b, (dims, ((), ())), precision=precision, preferred_element_type=F32)


def split(x):
    high = x.astype(BF16)
    low = (x - high.astype(F32)).astype(BF16)
    return high, low


def iota(shape, dim):
    return lax.broadcasted_iota(I32, shape, dim)


def spread(x):
    return jnp.broadcast_to(x, (BR, VEC))


def thirds(x):
    high = x.astype(BF16).astype(F32)
    rest = x - high
    mid = rest.astype(BF16).astype(F32)
    low = (rest - mid).astype(BF16).astype(F32)
    return high, mid, low


def outer(left, both):
    h, m, l = thirds(left)
    hh, mm, ll = thirds(both)
    a = jnp.concatenate([h, h, m, h, m, l], axis=0).astype(BF16)
    b = jnp.concatenate([hh, mm, hh, ll, mm, hh], axis=0).astype(BF16)
    return dot(a, b, ((0,), (0,)))


def panel(left, right, lo):
    sub = iota((BR, VEC), 0)
    cols = [spread(left[:, lo + j : lo + j + 1]) for j in range(BR)]
    block = [[spread(cols[j][i : i + 1, :]) for j in range(i + 1)] for i in range(BR)]
    rows_l = [spread(left[i : i + 1, :]) for i in range(BR)]
    rows_r = [spread(right[i : i + 1, :]) for i in range(BR)]
    for j in range(BR):
        pivot = block[j][j]
        inv = lax.rsqrt(pivot)
        rows_l[j] = rows_l[j] * inv
        rows_r[j] = rows_r[j] * inv
        below = [block[i][j] * inv if i > j else None for i in range(BR)]
        for i in range(j + 1, BR):
            for k in range(j + 1, i + 1):
                block[i][k] = block[i][k] - below[i] * below[k]
        for i in range(j + 1, BR):
            rows_l[i] = rows_l[i] - below[i] * rows_l[j]
            rows_r[i] = rows_r[i] - below[i] * rows_r[j]
    left, right = rows_l[0], rows_r[0]
    for j in range(1, BR):
        left = jnp.where(sub == j, rows_l[j], left)
        right = jnp.where(sub == j, rows_r[j], right)
    return left, right


def factor(work, r_out, inv_out):
    sub, lane = iota((BR, VEC), 0), iota((BR, VEC), 1)
    for lo in range(0, VEC, BR):
        hi = lo + BR
        left, right = panel(work[lo:hi, :VEC], work[lo:hi, VEC:], lo)
        r_out[lo:hi, :] = jnp.where(lane >= sub + lo, left, 0.0)
        inv_out[lo:hi, :] = right
        if hi < VEC:
            update = outer(left, jnp.concatenate([left, right], axis=1))
            work[hi:, :] = work[hi:, :] - update[hi:, :]


def kernel(
    tan, jac, codes, owners, q_out, r_out,
    jv, jhi, jlo, ext0, ext1, acc, amat, omv, idxv, idxs,
    gram, rsb, part, gyb, tot, gfull, work, linv, pk, arr,
    loc_sem, jac_sem, hsend, hrecv, ar_send, ar_recv, a2a_send, a2a_recv, idx_sem,
    far_x, farther_x, far_y, near_y,
):
    gx = lax.axis_index("gx")
    gy = lax.axis_index("gy")
    me = gx * GY + gy
    core = lax.rem(gy, 2)
    off, on = core, 1 - core
    gx_hi, gx_lo = lax.rem(gx + 1, GX), lax.rem(gx + GX - 1, GX)
    gy_off = lax.rem(gy + 2 * core - 1 + GY, GY)
    gy_on = lax.rem(gy + 1 - 2 * core + GY, GY)

    def halo(s, src, dst, who, role, half=None):
        if half is not None:
            rows = pl.ds(half * (CELL // 2), CELL // 2)
            src, dst = src.at[rows], dst.at[rows]
        part_no = half or 0
        return pltpu.make_async_remote_copy(
            src_ref=src, dst_ref=dst, send_sem=hsend.at[s, role, part_no],
            recv_sem=hrecv.at[s, role, part_no], device_id=who, device_id_type=MESH,
        )

    def own(s, ext, a, b):
        return tan.at[a * 2 + b] if s == 0 else ext.at[(1 + a) * 4 + 1 + b]

    def own_copies(s, ext):
        x_off, x_on = [
            [
                (
                    halo(s, own(s, ext, 1, col), ext.at[1 + col], (gx_hi, gy), k, half),
                    halo(s, own(s, ext, 0, col), ext.at[12 + 1 + col], (gx_lo, gy), 2 + k, half),
                )
                for half in halves
            ]
            for k, col, halves in ((0, off, (0, 1)), (1, on, (None,)))
        ]
        y_off = [
            halo(s, own(s, ext, a, off), ext.at[(1 + a) * 4 + 3 * on], (gx, gy_off), 4 + a)
            for a in range(2)
        ]
        y_on = [
            halo(s, own(s, ext, a, on), ext.at[(1 + a) * 4 + 3 * off], (gx, gy_on), 6 + a)
            for a in range(2)
        ]
        return x_off, x_on, y_off, y_on

    def corner_copies(s, ext):
        c_off = [
            [
                halo(
                    s, ext.at[12 * side + 1 + off], ext.at[12 * side + 3 * on], (gx, gy_off),
                    8 + side, half,
                )
                for side in range(2)
            ]
            for half in range(2)
        ]
        c_on = [
            halo(s, ext.at[12 * side + 1 + on], ext.at[12 * side + 3 * off], (gx, gy_on), 10 + side)
            for side in range(2)
        ]
        return c_off, c_on

    exts = (ext0, ext1)
    sent = []

    def along_x(step):
        return (lax.rem(gx + step + GX, GX), gy)

    def along_y(step):
        return (gx, lax.rem(gy + step + GY, GY))

    def greet(sem, who):
        for device in who:
            pl.semaphore_signal(sem, inc=1, device_id=device, device_id_type=MESH)

    barrier = pltpu.get_barrier_semaphore()
    greet(barrier, (along_x(1), along_x(-1), along_y(1), along_y(-1)))
    locals_ = [
        pltpu.make_async_copy(tan.at[c], ext0.at[(1 + c // 2) * 4 + 1 + c % 2], loc_sem.at[c])
        for c in range(4)
    ]
    own_copy = pltpu.make_async_copy(owners, omv, loc_sem.at[4])
    jac_copies = [
        pltpu.make_async_copy(jac.at[:, s], jv.at[s], jac_sem.at[s]) for s in range(SWEEPS)
    ]
    for copy in (*locals_, own_copy, *jac_copies):
        copy.start()
    pl.semaphore_wait(barrier, 4)

    x_off, x_on, y_off, y_on = own_copies(0, ext0)
    for copy in (*x_off[0], *x_off[1], *y_off, *x_on[0], *y_on):
        copy.start()

    def product(s, cell, slot, field):
        high, low = split(field)
        j_high = jhi[s, cell, slot]
        j_low = jlo[s, cell, slot]
        wide = dot(j_high, jnp.concatenate([high, low], axis=1))
        return wide[:, :VEC] + (wide[:, VEC:] + dot(j_low, high))

    def split_jacobians(s):
        def body(n, carry):
            cell, slot = lax.div(n, SLOTS), lax.rem(n, SLOTS)
            high, low = split(jv[s, cell, slot])
            jhi[s, cell, slot] = high
            jlo[s, cell, slot] = low
            return carry

        lax.fori_loop(0, 4 * SLOTS, body, 0)

    def own_terms(s, ext):
        def body(cell, carry):
            at = (1 + lax.div(cell, 2)) * 4 + 1 + lax.rem(cell, 2)
            acc[cell] = product(s, cell, 0, ext[at])
            return carry

        lax.fori_loop(0, 4, body, 0)

    def routing():
        ones = jnp.ones((32, VEC), BF16)
        mine = (omv[...] == me).astype(F32).astype(BF16)
        per_cell = dot(mine, ones).astype(BF16)
        cell = iota((TILES, 512), 1)
        tile_of = lax.shift_right_logical(cell, 5) * 8 + lax.shift_right_logical(cell & 15, 1)
        pick = (tile_of == iota((TILES, 512), 0)).astype(F32).astype(BF16)
        count = dot(pick, per_cell)
        rows, lanes = iota((TILES, TILES), 0), iota((TILES, TILES), 1)
        tri = (lanes <= rows).astype(F32).astype(BF16)
        ends = dot(tri, count.astype(BF16))
        places = lanes.astype(F32)
        before = (ends <= places).astype(F32)
        tile_at = jnp.sum(before, axis=0, keepdims=True)
        passed = jnp.sum(before * count, axis=0, keepdims=True)
        slot_at = jnp.clip(2.0 * tile_at + places[:1] - passed, 0.0, 2.0 * TILES - 1.0)
        diag = iota((32, 32), 0) == iota((32, 32), 1)
        stack = []
        for c in range(4):
            row = omv[pl.ds((2 * gx + c // 2) * 16 + 2 * gy + c % 2, 1), :].astype(F32)
            stack.append(jnp.where(diag, jnp.broadcast_to(row, (32, 32)), 0.0))
        owner_of = dot(jnp.concatenate(stack, axis=0).astype(BF16), ones)
        hit = owner_of == places
        order = rows.astype(F32)
        first = jnp.min(jnp.where(hit, order, float(BLK - 1)), axis=0, keepdims=True)
        last = jnp.max(jnp.where(hit, order, 0.0), axis=0, keepdims=True)
        table = jnp.concatenate([first, last, slot_at, jnp.zeros((5, VEC), F32)], axis=0)
        idxv[...] = table.astype(I32)
        copy = pltpu.make_async_copy(idxv, idxs, idx_sem)
        copy.start()
        return copy

    idx_copy = None
    for s in range(SWEEPS):
        ext = exts[s]
        sent += [*x_off[0], *x_off[1], *x_on[0], *y_off, *y_on]
        if s == 0:
            jac_copies[0].wait()
            split_jacobians(0)
            for copy in locals_:
                copy.wait()
        own_terms(s, ext)
        c_off, c_on = corner_copies(s, ext)
        for half in range(2):
            for copy in x_off[half]:
                copy.wait_recv()
            for copy in c_off[half]:
                copy.start()
        for copy in x_on[0]:
            copy.wait_recv()
        for copy in c_on:
            copy.start()
        if s == 0:
            greet(far_x, (along_x(2), along_x(-2)))
        else:
            pl.semaphore_wait(farther_x, 2)
            greet(near_y, (along_y(1), along_y(-1)))
        sent += [*c_off[0], *c_off[1], *c_on]
        if s == 0:
            jac_copies[1].wait()
            split_jacobians(1)
            own_copy.wait()
            idx_copy = routing()
        for copy in (*y_on, *y_off, *c_on, *c_off[0], *c_off[1]):
            copy.wait_recv()
        if s == 0:
            pl.semaphore_wait(far_x, 2)
            greet(farther_x, (along_x(4), along_x(-4)))
            greet(far_y, (along_y(2), along_y(-2)))
        else:
            pl.semaphore_wait(far_y, 2)
            pl.semaphore_wait(near_y, 2)

        if s == 0:
            x_off, x_on, y_off, y_on = own_copies(1, ext1)
        for n in range(4):
            a, b = n % 2, (off if n < 2 else on)
            cell = a * 2 + b
            total = acc[cell]
            for slot in range(1, SLOTS):
                code = codes[a, b, s, slot]
                live = jnp.where(code != 9, 1.0, 0.0).astype(F32)
                safe = jnp.where(code != 9, code, 4)
                step_x = lax.shift_right_logical(safe * 11, 5)
                step_y = safe - 3 * step_x
                field = ext[(a + step_x) * 4 + b + step_y] * live
                total = total + product(s, cell, slot, field)
            if s == 0:
                ext1[(1 + a) * 4 + 1 + b] = total
                if n == 1:
                    for copy in (*x_off[0], *x_off[1], *y_off):
                        copy.start()
                if n == 3:
                    for copy in (*x_on[0], *y_on):
                        copy.start()
            else:
                amat[pl.ds(cell * 32, 32)] = total.reshape(32, BR, VEC)

    rows_all = amat[...].reshape(4 * CELL, VEC)
    gram[...] = dot(rows_all, rows_all, ((0,), (0,)), FULL)
    share = VEC // GX

    def to_gx(step, src, dst, phase):
        k = lax.rem(gx + step, GX)
        return pltpu.make_async_remote_copy(
            src_ref=src(k), dst_ref=dst, send_sem=ar_send.at[phase], recv_sem=ar_recv.at[phase],
            device_id=(k, gy), device_id_type=MESH,
        )

    def wait_bytes(ref, sem):
        pltpu.make_async_copy(ref, ref, sem).wait()

    for step in range(1, GX):
        to_gx(step, lambda k: gram.at[pl.ds(k * share, share)], rsb.at[gx], 0).start()
    rsb[gx] = gram[pl.ds(gx * share, share), :]

    idx_copy.wait()

    def pack(o, carry):
        pk[o, 0] = amat[idxs[0, o] & (BLK - 1)]
        pk[o, 1] = amat[idxs[1, o] & (BLK - 1)]
        return carry

    near, away = (0, 1, GY - 1), tuple(range(2, GY - 1))

    def send(places):
        def body(turn, carry):
            to_x = (gx + 7 * turn) & (GX - 1)
            for step in places:
                to_y = (gy + step) & (GY - 1)
                pltpu.make_async_remote_copy(
                    src_ref=pk.at[to_x * GY + to_y], dst_ref=arr.at[me],
                    send_sem=a2a_send, recv_sem=a2a_recv,
                    device_id=(to_x, to_y), device_id_type=MESH,
                ).start()
            return carry

        return body

    lax.fori_loop(0, TILES, pack, 0, unroll=8)
    arr[me] = pk[me]
    send(near[1:])(0, 0)
    lax.fori_loop(1, CUTS[0], send(near), 0)
    wait_bytes(rsb.at[pl.ds(0, GX - 1)], ar_recv.at[0])
    mine = jnp.sum(rsb[...], axis=0)
    part[...] = mine
    for step in range(1, GY):
        pltpu.make_async_remote_copy(
            src_ref=part, dst_ref=gyb.at[gy], send_sem=ar_send.at[1], recv_sem=ar_recv.at[1],
            device_id=(gx, lax.rem(gy + step, GY)), device_id_type=MESH,
        ).start()
    gyb[gy] = mine
    lax.fori_loop(CUTS[0], GX, send(near), 0)
    lax.fori_loop(0, CUTS[1], send(away), 0)
    wait_bytes(gyb.at[pl.ds(0, GY - 1)], ar_recv.at[1])
    mine = jnp.sum(gyb[...], axis=0) * (1.0 / ROWS)
    tot[...] = mine
    for step in range(1, GX):
        to_gx(step, lambda k: tot, gfull.at[pl.ds(gx * share, share)], 2).start()
    gfull[pl.ds(gx * share, share), :] = mine
    lax.fori_loop(CUTS[1], CUTS[2], send(away), 0)
    wait_bytes(gfull.at[pl.ds(0, (GX - 1) * share)], ar_recv.at[2])
    lax.fori_loop(CUTS[2], GX, send(away), 0)

    eye = (iota((VEC, VEC), 0) == iota((VEC, VEC), 1)).astype(F32)
    work[:, :VEC] = gfull[...]
    work[:, VEC:] = eye
    factor(work, r_out, linv)

    wait_bytes(arr.at[pl.ds(0, TILES - 1)], a2a_recv)

    def unpack(p, carry):
        at = idxs[2, p] & (2 * TILES - 1)
        amat[p] = arr[lax.shift_right_logical(at, 1), at & 1]
        return carry

    lax.fori_loop(0, BLK, unpack, 0, unroll=8)
    rows_all = amat[...].reshape(4 * CELL, VEC)
    q_out[...] = dot(rows_all, linv[...], ((1,), (1,)), FULL).reshape(BLK, BR, VEC)

    for copy in sent:
        copy.wait_send()
    wait_bytes(rsb.at[pl.ds(0, GX - 1)], ar_send.at[0])
    wait_bytes(gyb.at[pl.ds(0, GY - 1)], ar_send.at[1])
    wait_bytes(gfull.at[pl.ds(0, (GX - 1) * share)], ar_send.at[2])
    wait_bytes(arr.at[pl.ds(0, TILES - 1)], a2a_send)


def shards(tangent, jacobians, partner_codes, owner_map):
    hbm = pl.BlockSpec(memory_space=pltpu.HBM)
    vmem = pl.BlockSpec(memory_space=pltpu.VMEM)
    cells = (4, CELL, VEC)
    return pl.pallas_call(
        kernel,
        out_shape=(
            jax.ShapeDtypeStruct((BLK, BR, VEC), F32),
            jax.ShapeDtypeStruct((VEC, VEC), F32),
        ),
        in_specs=[hbm, hbm, pl.BlockSpec(memory_space=pltpu.SMEM), hbm],
        out_specs=(vmem, vmem),
        scratch_shapes=[
            pltpu.VMEM((SWEEPS, 4, SLOTS, CELL, CELL), F32),
            pltpu.VMEM((SWEEPS, 4, SLOTS, CELL, CELL), BF16),
            pltpu.VMEM((SWEEPS, 4, SLOTS, CELL, CELL), BF16),
            pltpu.VMEM((16, CELL, VEC), F32),
            pltpu.VMEM((16, CELL, VEC), F32),
            pltpu.VMEM(cells, F32),
            pltpu.VMEM((BLK, BR, VEC), F32),
            pltpu.VMEM((512, 32), I32),
            pltpu.VMEM((8, VEC), I32),
            pltpu.SMEM((8, VEC), I32),
            pltpu.VMEM((VEC, VEC), F32),
            pltpu.VMEM((GX, VEC // GX, VEC), F32),
            pltpu.VMEM((VEC // GX, VEC), F32),
            pltpu.VMEM((GY, VEC // GX, VEC), F32),
            pltpu.VMEM((VEC // GX, VEC), F32),
            pltpu.VMEM((VEC, VEC), F32),
            pltpu.VMEM((VEC, 2 * VEC), F32),
            pltpu.VMEM((VEC, VEC), F32),
            pltpu.VMEM((TILES, 2, BR, VEC), F32),
            pltpu.VMEM((TILES, 2, BR, VEC), F32),
            pltpu.SemaphoreType.DMA((5,)),
            pltpu.SemaphoreType.DMA((SWEEPS,)),
            pltpu.SemaphoreType.DMA((SWEEPS, 12, 2)),
            pltpu.SemaphoreType.DMA((SWEEPS, 12, 2)),
            pltpu.SemaphoreType.DMA((3,)),
            pltpu.SemaphoreType.DMA((3,)),
            pltpu.SemaphoreType.DMA,
            pltpu.SemaphoreType.DMA,
            pltpu.SemaphoreType.DMA,
            pltpu.SemaphoreType.REGULAR,
            pltpu.SemaphoreType.REGULAR,
            pltpu.SemaphoreType.REGULAR,
            pltpu.SemaphoreType.REGULAR,
        ],
        compiler_params=pltpu.CompilerParams(
            collective_id=0, has_side_effects=True, vmem_limit_bytes=62 * 2**20
        ),
    )(
        tangent.reshape(cells),
        jacobians.reshape(4, SWEEPS, SLOTS, CELL, CELL),
        partner_codes,
        owner_map.reshape(-1, owner_map.shape[2]),
    )


def solution(mesh):
    return jax.shard_map(
        shards,
        mesh=mesh,
        in_specs=(
            P("gx", "gy", None, None),
            P("gx", "gy", None, None, None, None),
            P("gx", "gy", None, None),
            P(),
        ),
        out_specs=(P(("gx", "gy"), None, None), P()),
        check_vma=False,
    )
```
